256 devices in a mesh: row: 8 (over y, x_hi), col: 8 (over z), depth: 4 (over x_lo, core).
Axes of the slice: x: 4 (x_hi: 2, x_lo: 2; x = x_hi * 2 + x_lo), y: 4, z: 8, core: 2. Of those that a mesh axis runs over, the one named last changes fastest.
Arguments:
- inputs: bfloat16 [1024, 7168], P(('depth', 'col'), 'row'), may hold values from -6 to 6
- out_grad: bfloat16 [1024, 7168], P(('depth', 'col'), 'row'), may hold values from -6 to 6
- w_gate: bfloat16 [7168, 15360], P('row', 'col'), may hold values from -0.0625 to 0.0625
- w_up: bfloat16 [7168, 15360], P('row', 'col'), may hold values from -0.0625 to 0.0625
- w_down: bfloat16 [15360, 7168], P('col', 'row'), may hold values from -0.046875 to 0.046875
Outputs:
- input_grad: bfloat16 [1024, 7168], P(('depth', 'col'), 'row')
- gate_grad: bfloat16 [7168, 15360], P(('row', 'depth'), 'col')
- up_grad: bfloat16 [7168, 15360], P(('row', 'depth'), 'col')
- down_grad: bfloat16 [15360, 7168], P(('col', 'depth'), 'row')
The draws below stay inside these ranges and needn't reach their ends.
All inputs are finite; a program needn't handle non-finite values.
Results may differ from the reference program's by a relative error of at most 0.005.
Values may be sent and summed in bfloat16 or wider, within the bound.
A program may use at most 128 MiB of HBM per device.

```python
import jax
import jax.numpy as jnp

D = 7168
FF = 15360
TOKENS = 1024


def steps_of(key, shape, cuts, least, top_value):
    def one(dim, blocks):
        draws = jax.random.uniform(jax.random.fold_in(jax.random.fold_in(key, 6), dim), (blocks,), jnp.float32, least / len(cuts), top_value / len(cuts))
        return jnp.repeat(jnp.exp(draws), shape[dim] // blocks).reshape((-1,) + (1,) * (len(shape) - dim - 1))

    gain = one(*cuts[0])
    for cut in cuts[1:]:
        gain = gain * one(*cut)
    return gain


def centred(stream_key, dims, deviation, reach, shards=(), dtype=jnp.bfloat16):
    drawn = deviation * jax.random.normal(stream_key, dims, jnp.float32)
    if shards:
        drawn = drawn * steps_of(stream_key, dims, shards, -0.22, 0.18)
    return jnp.clip(drawn, -reach, reach).astype(dtype)


def setup_inputs(seed: int = 0) -> dict:
    seeds = jax.random.split(jax.random.key(seed), 6)
    return {
        "inputs": centred(seeds[0], (TOKENS, D), 1.0, 6.0, ((0, 32), (1, 8))),
        "out_grad": centred(seeds[1], (TOKENS, D), 1.0, 6.0, ((0, 32), (1, 8))),
        "w_gate": centred(seeds[2], (D, FF), D ** -0.5, 0.0625, ((0, 8), (1, 8))),
        "w_up": centred(seeds[3], (D, FF), D ** -0.5, 0.0625, ((0, 8), (1, 8))),
        "w_down": centred(seeds[4], (FF, D), FF ** -0.5, 0.046875, ((0, 8), (1, 8))),
    }


def reference(inputs, out_grad, w_gate, w_up, w_down):
    gate_val = jnp.dot(inputs, w_gate, preferred_element_type=jnp.float32)
    up_val = jnp.dot(inputs, w_up, preferred_element_type=jnp.float32)
    hidden_grad = jnp.dot(out_grad, w_down.T, preferred_element_type=jnp.float32)
    sigma = jax.nn.sigmoid(gate_val)
    hidden = (gate_val * sigma * up_val).astype(jnp.bfloat16)
    gate_back = (hidden_grad * up_val * sigma * (1.0 + gate_val * (1.0 - sigma))).astype(jnp.bfloat16)
    up_back = (hidden_grad * gate_val * sigma).astype(jnp.bfloat16)
    input_grad = jnp.dot(gate_back, w_gate.T, preferred_element_type=jnp.float32)
    input_grad = input_grad + jnp.dot(up_back, w_up.T, preferred_element_type=jnp.float32)
    gate_grad = jnp.dot(inputs.T, gate_back, preferred_element_type=jnp.float32)
    up_grad = jnp.dot(inputs.T, up_back, preferred_element_type=jnp.float32)
    down_grad = jnp.dot(hidden.T, out_grad, preferred_element_type=jnp.float32)
    return (input_grad.astype(jnp.bfloat16), gate_grad.astype(jnp.bfloat16),
            up_grad.astype(jnp.bfloat16), down_grad.astype(jnp.bfloat16))
```

```python
import jax
import jax.numpy as jnp
from jax import lax
from jax.experimental import pallas as pl
from jax.experimental.pallas import tpu as pltpu
from jax.sharding import PartitionSpec as P

MESH = pl.DeviceIdType.MESH
F32, BF16 = jnp.float32, jnp.bfloat16

DELTA = (0, 1, -1, 2, -2, 3, -3, 4)
SLOT = {1: 1, -1: 2, 2: 3, -2: 4, 3: 5, -3: 6, 4: 7, -4: 7}
DEEP = 4
STEPS = 8
ROWS = 32
WIDE = 896
FULL = 1920
OWN = 480
PAD = 512
WIN = 640
PIECE = 224


def mm(a, b):
    return lax.dot_general(a, b, (((1,), (0,)), ((), ())), preferred_element_type=F32)


def mm_t(a, b):
    return lax.dot_general(a, b, (((1,), (1,)), ((), ())), preferred_element_type=F32)


def kernel(
    x_hbm, dy_hbm, wg_hbm, wu_hbm, wd_hbm,
    ig_out, gu_out, down_out,
    xd, xt, win, w2, wd, part, part_own, psend, precv, ysum, xrecv, g,
    piece_send, piece_recv, down, ig, ig_core, ig_xs, ig_xr, ig_zs, ig_zr, ig_fin,
    load_sem, z_s, z_r, cf_s, cf_r, xf_s, xf_r, cb_s, cb_r, y_s, y_r, h_s, h_r,
    ah_s, ah_r, ay_s, ay_r, af_s, af_r, p_s, p_r, ic_s, ic_r, ix_s, ix_r, iz_s, iz_r, out_sem,
):
    row, z, dep = lax.axis_index("row"), lax.axis_index("col"), lax.axis_index("depth")
    y, xh = row // 2, row % 2
    xl, c = dep // 2, dep % 2
    dep_x = (1 - xl) * 2 + c
    dep_c = xl * 2 + 1 - c
    dep_xc = (1 - xl) * 2 + 1 - c

    def at_row(yy, hh):
        return {"row": yy * 2 + hh, "col": z, "depth": dep}

    def at_depth(d):
        return {"row": row, "col": z, "depth": d}

    def at_col(zz):
        return {"row": row, "col": zz, "depth": dep}

    def y_at(j):
        return at_row((y + j) % 4, xh)

    def remote(src, dst, ss, rs, dev):
        return pltpu.make_async_remote_copy(
            src_ref=src, dst_ref=dst, send_sem=ss, recv_sem=rs, device_id=dev, device_id_type=MESH
        )

    start = jnp.where(dep == 3, 1280, dep * 480 - (dep * 480) % 128)
    start = pl.multiple_of(start, 128)
    shift = dep * 480 - start
    loads = [
        pltpu.make_async_copy(x_hbm, xd.at[0, 0, dep], load_sem.at[0]),
        pltpu.make_async_copy(dy_hbm, xd.at[1, 0, dep], load_sem.at[1]),
        pltpu.make_async_copy(wg_hbm.at[:, pl.ds(start, WIN)], win.at[0], load_sem.at[2]),
        pltpu.make_async_copy(wu_hbm.at[:, pl.ds(start, WIN)], win.at[1], load_sem.at[3]),
        pltpu.make_async_copy(wd_hbm.at[pl.ds(dep * OWN, OWN)], wd.at[pl.ds(0, OWN)], load_sem.at[4]),
    ]
    for cp in loads:
        cp.start()

    barrier = pltpu.get_barrier_semaphore()
    peers = [at_depth(dep_x), at_depth(dep_c), at_depth(dep_xc)]
    peers += [at_col((z + m) % STEPS) for m in range(1, STEPS)]
    peers += [y_at(j) for j in (1, 2, 3)] + [at_row(y, 1 - xh)]
    for dev in peers:
        pl.semaphore_signal(barrier, inc=1, device_id=dev, device_id_type=MESH)
    pl.semaphore_wait(barrier, len(peers))

    loads[0].wait()
    loads[1].wait()

    def block(s, d):
        return xd.at[:, s, d]

    z_sends = []
    for m in (1, -1, 2, -2, 3, -3, 4):
        slot = SLOT[-m]
        z_sends.append(remote(block(0, dep), block(slot, dep), z_s.at[slot], z_r.at[slot], at_col((z + m + STEPS) % STEPS)))
    for cp in z_sends:
        cp.start()

    def to_core(s):
        return remote(block(s, dep), block(s, dep), cf_s.at[s], cf_r.at[s], at_depth(dep_c))

    def to_x(s):
        return remote(block(s, dep), block(s, dep), xf_s.at[s], xf_r.at[s], at_depth(dep_x))

    def x_to_core(s):
        return remote(block(s, dep_x), block(s, dep_x), cb_s.at[s], cb_r.at[s], at_depth(dep_c))

    def share(s):
        to_x(s).start()
        to_core(s).start()

    share(0)

    pick = (
        lax.broadcasted_iota(jnp.int32, (WIN, PAD), 0) - lax.broadcasted_iota(jnp.int32, (WIN, PAD), 1) == shift
    ) & (lax.broadcasted_iota(jnp.int32, (WIN, PAD), 1) < OWN)
    pick = jnp.where(pick, 1.0, 0.0).astype(BF16)
    for i in range(2):
        loads[2 + i].wait()

        def select(t, carry, i=i):
            r = pl.ds(pl.multiple_of(t * 224, 32), 224)
            cut = mm(win[i, r], pick).astype(BF16)
            for k in range(2):
                w2[k, r, i * 256 : (i + 1) * 256] = cut[:, k * 256 : (k + 1) * 256]
            return carry

        lax.fori_loop(0, 4, select, 0)
    loads[4].wait()
    wd[OWN:PAD, :] = jnp.zeros((PAD - OWN, WIDE), BF16)

    def y_send(s, j):
        d = (y + 4 - j) % 4
        return remote(psend.at[s, d], precv.at[s, j - 1], y_s.at[s, j - 1], y_r.at[s, j - 1], at_row(d, xh))

    def x_send(s):
        return remote(ysum.at[s, 1 - xh], xrecv.at[s], h_s.at[s], h_r.at[s], at_row(y, 1 - xh))

    def stage_products(s):
        to_core(s).wait_recv()
        x_to_core(s).wait_recv()
        xs = xd[0, s].reshape(DEEP * ROWS, WIDE)
        ds = xd[1, s].reshape(DEEP * ROWS, WIDE)
        for k in range(3):
            lanes = slice(k * PAD, (k + 1) * PAD)
            p = mm(xs, w2[k]) if k < 2 else mm_t(ds, wd[...])
            p = p.reshape(DEEP, ROWS, PAD)
            part[:, :, lanes] = p
            psend[s, :, :, lanes] = p.astype(BF16)
        for j in (2, 1, 3):
            y_send(s, j).start()
        part_own[s] = part[y]
        xt[:, :, pl.ds(pl.multiple_of(s * 128, 128), 128)] = xs.T.reshape(DEEP, PIECE, 128)

    def stage_y(s):
        total = part_own[s]
        for j in (1, 3, 2):
            y_send(s, j).wait_recv()
            total = total + precv[s, j - 1].astype(F32)
        ysum[s] = total.reshape(2, ROWS // 2, 3 * PAD)
        x_send(s).start()

    def stage_x(s):
        x_send(s).wait_recv()
        total = ysum[s, xh] + xrecv[s]
        for k in range(2):
            gate = total[:, k * PAD : k * PAD + 256]
            up = total[:, k * PAD + 256 : (k + 1) * PAD]
            back = total[:, 2 * PAD + k * 256 : 2 * PAD + (k + 1) * 256]
            sigma = jax.nn.sigmoid(gate)
            g[2, s, y, xh, :, k * 256 : (k + 1) * 256] = (gate * sigma * up).astype(BF16)
            g[k, s, y, xh, :, 0:256] = (back * up * sigma * (1.0 + gate * (1.0 - sigma))).astype(BF16)
            g[k, s, y, xh, :, 256:512] = (back * gate * sigma).astype(BF16)

    def step(it, carry):
        @pl.when((it >= 1) & (it < STEPS))
        def _():
            remote(block(0, dep), block(it, dep), z_s.at[it], z_r.at[it], at_col(z)).wait_recv()
            share(it)

        @pl.when((it >= 1) & (it < STEPS + 1))
        def _():
            s = it - 1
            to_x(s).wait_recv()
            x_to_core(s).start()

        @pl.when((it >= 2) & (it < STEPS + 2))
        def _():
            stage_products(it - 2)

        @pl.when((it >= 4) & (it < STEPS + 4))
        def _():
            stage_y(it - 4)

        @pl.when(it >= 5)
        def _():
            stage_x(it - 5)

        return carry

    lax.fori_loop(0, STEPS + 5, step, 0)

    def ag_x(k):
        return remote(g.at[k, :, y, xh], g.at[k, :, y, xh], ah_s.at[k], ah_r.at[k], at_row(y, 1 - xh))

    def ag_y(k, j):
        return remote(g.at[k, :, y, xh], g.at[k, :, y, xh], ay_s.at[k, j - 1], ay_r.at[k, j - 1], at_row((y + 4 - j) % 4, xh))

    def ag_f(k, j):
        src = g.at[k, :, y, 1 - xh]
        return remote(src, src, af_s.at[k, j - 1], af_r.at[k, j - 1], at_row((y + 4 - j) % 4, xh))

    for k in range(3):
        ag_x(k).start()
    for k in range(3):
        for j in (2, 1, 3):
            ag_y(k, j).start()
        ag_x(k).wait_recv()
        for j in (2, 1, 3):
            ag_f(k, j).start()

    def ag_wait(k):
        for j in (1, 2, 3):
            ag_y(k, j).wait_recv()
            ag_f(k, j).wait_recv()

    def piece(k, j):
        return remote(piece_send.at[k, j], piece_recv.at[k, j], p_s.at[k, j], p_r.at[k, j], at_depth((dep + j) % DEEP))

    for k in range(2):
        ag_wait(k)
        gk = g[k].reshape(1024, PAD)
        for j in (2, 1, 3, 0):
            rows = mm(xt[(dep + j) % DEEP], gk).astype(BF16)
            if j:
                piece_send[k, j] = rows
                piece(k, j).start()
            else:
                piece_recv[k, 0] = rows

    def ig_step(s, carry):
        r = mm_t(g[0, s].reshape(128, PAD), w2[0]) + mm_t(g[1, s].reshape(128, PAD), w2[1])
        r = r.reshape(2, 2, ROWS, WIDE)
        for a in range(2):
            for b in range(2):
                ig[b, a, s] = r[a, b]
        return carry

    lax.fori_loop(0, STEPS, ig_step, 0)
    ig_c = remote(ig.at[1 - c], ig_core, ic_s, ic_r, at_depth(dep_c))
    ig_c.start()

    ag_wait(2)

    def down_step(t, carry):
        lanes = pl.ds(pl.multiple_of(t * 128, 128), 128)
        h = g[2, :, :, :, :, lanes].reshape(1024, 128)
        r = lax.dot_general(h, xd[1].reshape(1024, WIDE), (((0,), (0,)), ((), ())), preferred_element_type=F32)
        down[pl.ds(pl.multiple_of(t * 128, 128), 128), :] = r.astype(BF16)
        return carry

    lax.fori_loop(0, 4, down_step, 0)
    down_copy = pltpu.make_async_copy(down.at[pl.ds(0, OWN)], down_out, out_sem.at[0])
    down_copy.start()

    ig_c.wait_recv()
    ig_xs[...] = (ig[c, 1 - xl] + ig_core[1 - xl]).astype(BF16)
    ig_x = remote(ig_xs, ig_xr, ix_s, ix_r, at_depth(dep_x))
    ig_x.start()
    ig_fin[...] = ig[c, xl] + ig_core[xl]
    ig_x.wait_recv()
    ig_fin[...] = ig_fin[...] + ig_xr[...].astype(F32)
    ig_zs[...] = ig_fin[...].astype(BF16)
    ig_sends = []
    for s in range(1, STEPS):
        cp = remote(ig_zs.at[s], ig_zr.at[s], iz_s.at[s], iz_r.at[s], at_col((z + DELTA[s] + STEPS) % STEPS))
        cp.start()
        ig_sends.append(cp)
    total = ig_fin[0]
    for s in range(1, STEPS):
        ig_sends[s - 1].wait_recv()
        total = total + ig_zr[s].astype(F32)
    ig_zs[0] = total.astype(BF16)
    ig_copy = pltpu.make_async_copy(ig_zs.at[0], ig_out, out_sem.at[1])
    ig_copy.start()

    for k in range(2):
        for j in (1, 2, 3):
            piece(k, j).wait_recv()
    gu_copies = []
    for k in range(2):
        for j in range(DEEP):
            src = (dep + DEEP - j) % DEEP
            gu_copies.append(pltpu.make_async_copy(piece_recv.at[k, j], gu_out.at[k, src], out_sem.at[2 + k * DEEP + j]))
    for cp in gu_copies:
        cp.start()

    for cp in z_sends:
        cp.wait_send()

    def drain(s, carry):
        to_core(s).wait_send()
        to_x(s).wait_send()
        x_to_core(s).wait_send()
        for j in (1, 2, 3):
            y_send(s, j).wait_send()
        x_send(s).wait_send()
        return carry

    lax.fori_loop(0, STEPS, drain, 0)
    for k in range(3):
        ag_x(k).wait_send()
        for j in (1, 2, 3):
            ag_y(k, j).wait_send()
            ag_f(k, j).wait_send()
    for k in range(2):
        for j in (1, 2, 3):
            piece(k, j).wait_send()
    ig_c.wait_send()
    ig_x.wait_send()
    for cp in ig_sends:
        cp.wait_send()
    down_copy.wait()
    ig_copy.wait()
    for cp in gu_copies:
        cp.wait()


def on_device(inputs, out_grad, w_gate, w_up, w_down):
    vm = pltpu.VMEM
    dma = pltpu.SemaphoreType.DMA
    anyspace = pl.BlockSpec(memory_space=pl.ANY)
    half = ROWS // 2
    ig, gu, down = pl.pallas_call(
        kernel,
        out_shape=(
            jax.ShapeDtypeStruct((ROWS, WIDE), BF16),
            jax.ShapeDtypeStruct((2, DEEP, PIECE, PAD), BF16),
            jax.ShapeDtypeStruct((OWN, WIDE), BF16),
        ),
        in_specs=[anyspace] * 5,
        out_specs=(anyspace,) * 3,
        scratch_shapes=[
            vm((2, STEPS, DEEP, ROWS, WIDE), BF16),
            vm((DEEP, PIECE, 1024), BF16),
            vm((2, WIDE, WIN), BF16),
            vm((2, WIDE, PAD), BF16),
            vm((PAD, WIDE), BF16),
            vm((DEEP, ROWS, 3 * PAD), F32),
            vm((STEPS, ROWS, 3 * PAD), F32),
            vm((STEPS, DEEP, ROWS, 3 * PAD), BF16),
            vm((STEPS, 3, ROWS, 3 * PAD), BF16),
            vm((STEPS, 2, half, 3 * PAD), F32),
            vm((STEPS, half, 3 * PAD), F32),
            vm((3, STEPS, 4, 2, half, PAD), BF16),
            vm((2, DEEP, PIECE, PAD), BF16),
            vm((2, DEEP, PIECE, PAD), BF16),
            vm((PAD, WIDE), BF16),
            vm((2, 2, STEPS, ROWS, WIDE), F32),
            vm((2, STEPS, ROWS, WIDE), F32),
            vm((STEPS, ROWS, WIDE), BF16),
            vm((STEPS, ROWS, WIDE), BF16),
            vm((STEPS, ROWS, WIDE), BF16),
            vm((STEPS, ROWS, WIDE), BF16),
            vm((STEPS, ROWS, WIDE), F32),
            dma((5,)),
            dma((8,)), dma((8,)),
            dma((8,)), dma((8,)),
            dma((8,)), dma((8,)),
            dma((8,)), dma((8,)),
            dma((8, 3)), dma((8, 3)),
            dma((8,)), dma((8,)),
            dma((3,)), dma((3,)),
            dma((3, 3)), dma((3, 3)),
            dma((3, 3)), dma((3, 3)),
            dma((2, 4)), dma((2, 4)),
            dma, dma,
            dma, dma,
            dma((8,)), dma((8,)),
            dma((10,)),
        ],
        compiler_params=pltpu.CompilerParams(
            collective_id=0, has_side_effects=True, vmem_limit_bytes=60 * 1024 * 1024
        ),
        cost_estimate=pl.CostEstimate(flops=8 * 10**9, bytes_accessed=12 * 10**6, transcendentals=10**6),
        name="ffn_backward",
    )(inputs, out_grad, w_gate, w_up, w_down)

    gu = gu.transpose(2, 1, 0, 3)
    gate = gu[..., :256].reshape(PIECE, DEEP, PAD)[..., :OWN].reshape(PIECE, FULL)
    up = gu[..., 256:].reshape(PIECE, DEEP, PAD)[..., :OWN].reshape(PIECE, FULL)
    return ig, gate, up, down


def solution(mesh):
    placed = (
        P(("depth", "col"), "row"),
        P(("depth", "col"), "row"),
        P("row", "col"),
        P("row", "col"),
        P("col", "row"),
    )
    return jax.shard_map(
        on_device,
        mesh=mesh,
        in_specs=placed,
        out_specs=(
            P(("depth", "col"), "row"),
            P(("row", "depth"), "col"),
            P(("row", "depth"), "col"),
            P(("col", "depth"), "row"),
        ),
        check_vma=False,
    )
```

```python
import jax
import jax.numpy as jnp
from jax import lax
from jax.experimental import pallas as pl
from jax.experimental.pallas import tpu as pltpu
from jax.sharding import PartitionSpec as P

MESH = pl.DeviceIdType.MESH
F32, BF16 = jnp.float32, jnp.bfloat16

DELTA = (0, 1, -1, 2, -2, 3, -3, 4)
DEEP = 4
STEPS = 8
ROWS = 32
WIDE = 896
FULL = 1920
OWN = 480
PAD = 512
WIN = 640
PIECE = 224
HALF = ROWS // 2
CUT = 128
GU = 4
CHUNKS = 6
LANES = 2 * CUT
SUMS = 3 * PAD
GROUPS = ((0, 1), (1, 3), (3, 5), (5, 7), (7, 8))
PARTS = tuple((k, 0, 5) for k in range(4)) + tuple((k, 5, 8) for k in range(4)) + ((4, 0, 8), (5, 0, 8))


def mm(a, b):
    return lax.dot_general(a, b, (((1,), (0,)), ((), ())), preferred_element_type=F32)


def mm_t(a, b):
    return lax.dot_general(a, b, (((1,), (1,)), ((), ())), preferred_element_type=F32)


def kernel(
    x_hbm, dy_hbm, wg_hbm, wu_hbm, wd_hbm,
    ig_out, gate_out, up_out, down_out,
    xd, xt, win, w2, w2t, wd, part, part_own, psend, precv, ysum, xrecv, g,
    piece_send, piece_recv, gate_fin, up_fin, down, ig, ig_core, ig_xs, ig_xr, ig_zs, ig_zr, ig_fin, ig_res,
    load_sem, zo_s, zo_r, zf_s, zf_r, co_s, co_r, cf_s, cf_r, x0_s, x0_r, y_s, y_r, h_s, h_r,
    ah_s, ah_r, ay_s, ay_r, af_s, af_r, p_s, p_r, ic_s, ic_r, ix_s, ix_r, iz_s, iz_r, out_sem,
):
    row, z, dep = lax.axis_index("row"), lax.axis_index("col"), lax.axis_index("depth")
    y, xh = row // 2, row % 2
    xl, c = dep // 2, dep % 2
    dep_x = (1 - xl) * 2 + c
    dep_c = xl * 2 + 1 - c
    dep_xc = (1 - xl) * 2 + 1 - c
    y_up, y_down = (y + 1) % 4, (y + 3) % 4

    def at_row(yy, hh):
        return {"row": yy * 2 + hh, "col": z, "depth": dep}

    def at_depth(d):
        return {"row": row, "col": z, "depth": d}

    def at_col(zz):
        return {"row": row, "col": zz, "depth": dep}

    x_peer = at_row(y, 1 - xh)

    def remote(src, dst, ss, rs, dev):
        return pltpu.make_async_remote_copy(
            src_ref=src, dst_ref=dst, send_sem=ss, recv_sem=rs, device_id=dev, device_id_type=MESH
        )

    start = jnp.where(dep == 3, 1280, dep * 480 - (dep * 480) % 128)
    start = pl.multiple_of(start, 128)
    shift = dep * 480 - start
    loads = [
        pltpu.make_async_copy(x_hbm, xd.at[0, 0, xl, c], load_sem.at[0]),
        pltpu.make_async_copy(dy_hbm, xd.at[1, 0, xl, c], load_sem.at[1]),
        pltpu.make_async_copy(wg_hbm.at[:, pl.ds(start, WIN)], win.at[0], load_sem.at[2]),
        pltpu.make_async_copy(wu_hbm.at[:, pl.ds(start, WIN)], win.at[1], load_sem.at[3]),
        pltpu.make_async_copy(wd_hbm.at[pl.ds(dep * OWN, OWN)], wd.at[pl.ds(0, OWN)], load_sem.at[4]),
    ]
    for cp in loads:
        cp.start()

    barrier = pltpu.get_barrier_semaphore()
    peers = [at_depth(dep_x), at_depth(dep_c), at_depth(dep_xc)]
    peers += [at_col((z + m) % STEPS) for m in range(1, STEPS)]
    peers += [at_row((y + m) % 4, xh) for m in (1, 2, 3)] + [x_peer]
    peers += [{"row": row, "col": (z + m) % STEPS, "depth": dep_x} for m in (1, STEPS - 1)]
    for dev in peers:
        pl.semaphore_signal(barrier, inc=1, device_id=dev, device_id_type=MESH)

    pick = (
        lax.broadcasted_iota(jnp.int32, (WIN, PAD), 0) - lax.broadcasted_iota(jnp.int32, (WIN, PAD), 1) == shift
    ) & (lax.broadcasted_iota(jnp.int32, (WIN, PAD), 1) < OWN)
    pick = jnp.where(pick, 1.0, 0.0).astype(BF16)

    def select(i):
        loads[2 + i].wait()

        def one(t, carry):
            r = pl.ds(pl.multiple_of(t * 224, 32), 224)
            cut = mm(win[i, r], pick).astype(BF16)
            for k in range(GU):
                w2[r, k * LANES + i * CUT : k * LANES + (i + 1) * CUT] = cut[:, k * CUT : (k + 1) * CUT]
            return carry

        lax.fori_loop(0, 4, one, 0)

    select(0)
    loads[0].wait()
    loads[1].wait()
    pl.semaphore_wait(barrier, len(peers))

    def block(s, a, b):
        return xd.at[:, s, a, b]

    def ring(s, a, ss, rs):
        to = (z + STEPS - 1) % STEPS if s % 2 else (z + 1) % STEPS
        return remote(block(max(s - 2, 0), a, c), block(s, a, c), ss.at[s], rs.at[s], at_col(to))

    def ring_last(a, ss, rs, i):
        to = (z + 1) % STEPS if i == 0 else (z + STEPS - 1) % STEPS
        src = 6 if i == 0 else 5
        return remote(xd.at[i, src, a, c], xd.at[i, 7, a, c], ss.at[7 + i], rs.at[7 + i], at_col(to))

    def to_core(s, a, ss, rs):
        return remote(block(s, a, c), block(s, a, c), ss.at[s], rs.at[s], at_depth(dep_c))

    def to_x():
        return remote(block(0, xl, c), block(0, xl, c), x0_s, x0_r, at_depth(dep_x))

    def diagonal(s):
        to = (z + STEPS - 1) % STEPS if s == 1 else (z + 1) % STEPS
        dev = {"row": row, "col": to, "depth": dep_x}
        return remote(block(0, xl, c), block(s, xl, c), zf_s.at[s], zf_r.at[s], dev)

    to_x().start()
    ring(1, xl, zo_s, zo_r).start()
    ring(2, xl, zo_s, zo_r).start()
    diagonal(1).start()
    diagonal(2).start()
    to_core(0, xl, co_s, co_r).start()

    select(1)
    loads[4].wait()
    wd[OWN:PAD, :] = jnp.zeros((PAD - OWN, WIDE), BF16)

    def arrive_pair(m, a, zs, zr, cs, cr):
        for s in (2 * m - 1, 2 * m):
            ring(s, a, zs, zr).wait_recv()
            if m < 3:
                ring(s + 2, a, zs, zr).start()
            else:
                ring_last(a, zs, zr, s % 2).start()
        for s in (2 * m - 1, 2 * m):
            to_core(s, a, cs, cr).start()

    def arrive_last(a, zs, zr, cs, cr):
        ring_last(a, zs, zr, 0).wait_recv()
        ring_last(a, zs, zr, 1).wait_recv()
        to_core(7, a, cs, cr).start()

    own_sems = (zo_s, zo_r, co_s, co_r)
    far_sems = (zf_s, zf_r, cf_s, cf_r)

    def y_send(q, j):
        d = (y + 4 - j) % 4
        rows = pl.ds(GROUPS[q][0], GROUPS[q][1] - GROUPS[q][0])
        return remote(psend.at[d, rows], precv.at[j - 1, rows], y_s.at[q, j - 1], y_r.at[q, j - 1], at_row(d, xh))

    def x_send(q):
        rows = pl.ds(GROUPS[q][0], GROUPS[q][1] - GROUPS[q][0])
        return remote(ysum.at[1 - xh, rows], xrecv.at[rows], h_s.at[q], h_r.at[q], x_peer)

    def ag_x(q):
        lo, hi = GROUPS[q]
        rows = g.at[:, lo:hi, y, xh]
        return remote(rows, rows, ah_s.at[q], ah_r.at[q], x_peer)

    def ag_x_wait(q):
        lo, hi = GROUPS[q]
        rows = g.at[:, lo:hi, y, 1 - xh]
        remote(rows, rows, ah_s.at[q], ah_r.at[q], x_peer).wait_recv()

    def stage_products(q):
        lo, hi = GROUPS[q]
        n = hi - lo
        for s in range(lo, hi):
            to_core(s, xl, co_s, co_r).wait_recv()
            to_core(s, 1 - xl, cf_s, cf_r).wait_recv()
        xs = xd[0, lo:hi].reshape(n * 128, WIDE)
        ds = xd[1, lo:hi].reshape(n * 128, WIDE)
        for a, b, p in ((0, 2 * PAD, mm(xs, w2[...])), (2 * PAD, SUMS, mm_t(ds, wd[...]))):
            p = p.reshape(n, DEEP, ROWS, b - a)
            for s in range(n):
                part[:, s, :, a:b] = p[s]
                psend[:, lo + s, :, a:b] = p[s].astype(BF16)
        for j in (2, 1, 3):
            y_send(q, j).start()
        part_own[lo:hi] = part[y, 0:n]
        for s in range(lo, hi):
            xt[:, :, s * 128 : (s + 1) * 128] = xd[0, s].reshape(128, WIDE).T.reshape(DEEP, PIECE, 128)

    def stage_y(q):
        lo, hi = GROUPS[q]
        for j in (1, 3, 2):
            y_send(q, j).wait_recv()
        for s in range(lo, hi):
            total = part_own[s]
            for j in (1, 3, 2):
                total = total + precv[j - 1, s].astype(F32)
            total = total.reshape(2, HALF, SUMS)
            ysum[0, s] = total[0]
            ysum[1, s] = total[1]
        x_send(q).start()

    def stage_x(q):
        lo, hi = GROUPS[q]
        x_send(q).wait_recv()
        for s in range(lo, hi):
            total = ysum[xh, s] + xrecv[s]
            for k in range(GU):
                gate = total[:, k * LANES : k * LANES + CUT]
                up = total[:, k * LANES + CUT : (k + 1) * LANES]
                back = total[:, 2 * PAD + k * CUT : 2 * PAD + (k + 1) * CUT]
                sigma = jax.nn.sigmoid(gate)
                lanes = slice((k % 2) * CUT, (k % 2 + 1) * CUT)
                g[GU + k // 2, s, y, xh, :, lanes] = (gate * sigma * up).astype(BF16)
                g[k, s, y, xh, :, 0:CUT] = (back * up * sigma * (1.0 + gate * (1.0 - sigma))).astype(BF16)
                g[k, s, y, xh, :, CUT:LANES] = (back * gate * sigma).astype(BF16)
        ag_x(q).start()

    def ag_own(p, up):
        k, lo, hi = PARTS[p]
        rows = g.at[k, lo:hi, y]
        i = 0 if up else 1
        return remote(rows, rows, ay_s.at[p, i], ay_r.at[p, i], at_row(y_up if up else y_down, xh))

    def ag_own_wait(p, up):
        k, lo, hi = PARTS[p]
        rows = g.at[k, lo:hi, y_down if up else y_up]
        i = 0 if up else 1
        remote(rows, rows, ay_s.at[p, i], ay_r.at[p, i], at_row(y_up, xh)).wait_recv()

    def ag_pass(p, up):
        k, lo, hi = PARTS[p]
        i = 0 if up else 1
        rows = g.at[k, lo:hi, y_down if up else y_up, i]
        return remote(rows, rows, af_s.at[p, i], af_r.at[p, i], at_row(y_up if up else y_down, xh))

    def ag_pass_wait(p, up):
        k, lo, hi = PARTS[p]
        i = 0 if up else 1
        rows = g.at[k, lo:hi, (y + 2) % 4, i]
        remote(rows, rows, af_s.at[p, i], af_r.at[p, i], at_row(y_up, xh)).wait_recv()

    def ag_start(p):
        for up in (True, False):
            ag_own(p, up).start()

    def ag_middle(p):
        for up in (True, False):
            ag_own_wait(p, up)
            ag_pass(p, up).start()

    def ag_end(p):
        for up in (True, False):
            ag_pass_wait(p, up)

    src = block(0, 1 - xl, c)
    remote(src, src, x0_s, x0_r, at_depth(dep_x)).wait_recv()
    to_core(0, 1 - xl, cf_s, cf_r).start()
    arrive_pair(1, xl, *own_sems)
    stage_products(0)
    arrive_pair(1, 1 - xl, *far_sems)
    arrive_pair(2, xl, *own_sems)
    stage_products(1)
    arrive_pair(2, 1 - xl, *far_sems)
    arrive_pair(3, xl, *own_sems)
    stage_y(0)
    stage_products(2)
    arrive_pair(3, 1 - xl, *far_sems)
    arrive_last(xl, *own_sems)
    stage_x(0)
    stage_products(3)
    stage_y(1)
    arrive_last(1 - xl, *far_sems)
    stage_products(4)
    stage_x(1)
    stage_y(2)
    for k in range(GU):
        w2t[k * LANES : (k + 1) * LANES, :] = w2[:, k * LANES : (k + 1) * LANES].T
    stage_x(2)
    stage_y(3)
    for q in range(3):
        ag_x_wait(q)
    for p in range(4):
        ag_start(p)
    stage_x(3)
    stage_y(4)
    for p in range(4):
        ag_middle(p)
    stage_x(4)
    for q in (3, 4):
        ag_x_wait(q)

    def piece(k, j):
        d = (dep + j) % DEEP
        return remote(piece_send.at[k, d], piece_recv.at[k, dep], p_s.at[k, j], p_r.at[k, j], at_depth(d))

    def piece_wait(k, j):
        dst = piece_recv.at[k, (dep + DEEP - j) % DEEP]
        remote(dst, dst, p_s.at[k, j], p_r.at[k, j], at_depth(dep_x)).wait_recv()

    def pieces(k):
        gk = g[k].reshape(1024, LANES)
        piece_send[k] = mm(xt[...].reshape(WIDE, 1024), gk).astype(BF16).reshape(DEEP, PIECE, LANES)

    def pieces_start(k):
        for j in (2, 1, 3):
            piece(k, j).start()
        piece_recv[k, dep] = piece_send[k, dep]

    def ig_group(q):
        lo, hi = GROUPS[q]
        r = 0.0
        for k in range(GU):
            r = r + mm(g[k, lo:hi].reshape((hi - lo) * 128, LANES), w2t[k * LANES : (k + 1) * LANES, :])
        r = r.reshape(hi - lo, 2, 2, ROWS, WIDE)
        for s in range(lo, hi):
            for a in range(2):
                for b in range(2):
                    ig[b, a, s] = r[s - lo, a, b]
        ig_c(q).start()

    def ig_c(q):
        lo, hi = GROUPS[q]
        return remote(ig.at[1 - c, :, lo:hi], ig_core.at[:, lo:hi], ic_s.at[q], ic_r.at[q], at_depth(dep_c))

    def ig_z(s):
        return remote(ig_zs.at[s], ig_zr.at[s], iz_s.at[s], iz_r.at[s], at_col((z + DELTA[s] + STEPS) % STEPS))

    def ig_chip(q):
        lo, hi = GROUPS[q]
        ig_c(q).wait_recv()
        for s in range(lo, hi):
            total = ig[c, :, s] + ig_core[:, s]
            if s:
                ig_zs[s] = total.astype(BF16)
                ig_z(s).start()
            else:
                ig_fin[...] = total

    for p in range(4, 8):
        ag_start(p)
    for p in range(4):
        ag_end(p)
    for q in (2, 1, 0):
        ig_group(q)
    ag_middle(4)
    ag_start(8)
    ag_middle(5)
    ag_start(9)
    ig_chip(2)
    ag_middle(6)
    ag_middle(7)
    ag_end(4)
    pieces(0)
    pieces_start(0)
    ig_chip(1)
    ig_chip(0)
    ag_end(5)
    pieces(1)
    pieces_start(1)
    ag_end(6)
    ag_end(7)
    ig_group(4)
    ig_group(3)
    ag_middle(8)
    ag_middle(9)
    pieces(2)
    pieces_start(2)
    ig_chip(4)
    ig_chip(3)
    pieces(3)
    pieces_start(3)

    ag_end(8)
    ag_end(9)

    def down_step(t, carry):
        h = g[GU + t].reshape(1024, LANES)
        r = lax.dot_general(h, xd[1].reshape(1024, WIDE), (((0,), (0,)), ((), ())), preferred_element_type=F32)
        down[pl.ds(pl.multiple_of(t * LANES, LANES), LANES), :] = r.astype(BF16)
        return carry

    lax.fori_loop(0, 2, down_step, 0)
    outs = [pltpu.make_async_copy(down.at[pl.ds(0, OWN)], down_out, out_sem.at[0])]
    outs[0].start()

    def assemble(k):
        for j in (1, 2, 3):
            piece_wait(k, j)
        wide = min(CUT, OWN - k * CUT)
        for src in range(DEEP):
            lanes = slice(src * OWN + k * CUT, src * OWN + k * CUT + wide)
            gate_fin[:, lanes] = piece_recv[k, src, :, 0:wide]
            up_fin[:, lanes] = piece_recv[k, src, :, CUT : CUT + wide]

    assemble(0)
    assemble(1)
    total = ig_fin[...]
    for s in range(1, STEPS):
        ig_z(s).wait_recv()
        total = total + ig_zr[s].astype(F32)
    ig_fin[...] = total

    ig_xs[...] = ig_fin[1 - xl].astype(BF16)
    ig_x = remote(ig_xs, ig_xr, ix_s, ix_r, at_depth(dep_x))
    ig_x.start()
    assemble(2)
    ig_x.wait_recv()
    ig_res[...] = (ig_fin[xl] + ig_xr[...].astype(F32)).astype(BF16)
    outs.append(pltpu.make_async_copy(ig_res, ig_out, out_sem.at[3]))
    outs[-1].start()
    assemble(3)
    for i, (src, dst) in enumerate(((gate_fin, gate_out), (up_fin, up_out))):
        outs.append(pltpu.make_async_copy(src, dst, out_sem.at[1 + i]))
        outs[-1].start()

    to_x().wait_send()
    diagonal(1).wait_send()
    diagonal(2).wait_send()
    for a, zs, zr, cs, cr in ((xl, *own_sems), (1 - xl, *far_sems)):
        ring_last(a, zs, zr, 0).wait_send()
        ring_last(a, zs, zr, 1).wait_send()

        for s in range(1 if zs is zo_s else 3, 7):
            ring(s, a, zs, zr).wait_send()
        for s in range(STEPS):
            to_core(s, a, cs, cr).wait_send()

    for q in range(len(GROUPS)):
        for j in (1, 2, 3):
            y_send(q, j).wait_send()
        x_send(q).wait_send()
        ag_x(q).wait_send()
    for p in range(len(PARTS)):
        for up in (True, False):
            ag_own(p, up).wait_send()
            ag_pass(p, up).wait_send()
    for k in range(GU):
        for j in (1, 2, 3):
            piece(k, j).wait_send()
    for q in range(len(GROUPS)):
        ig_c(q).wait_send()
    ig_x.wait_send()
    for s in range(1, STEPS):
        ig_z(s).wait_send()
    for cp in outs:
        cp.wait()


def hand_on(a0, a1, a2, a3, b0, b1, b2, b3, sems):
    copies = [
        pltpu.make_async_copy(a, b, sems.at[i]) for i, (a, b) in enumerate(((a0, b0), (a1, b1), (a2, b2), (a3, b3)))
    ]
    for cp in copies:
        cp.start()
    for cp in copies:
        cp.wait()


def on_device(inputs, out_grad, w_gate, w_up, w_down):
    vm = pltpu.VMEM
    dma = pltpu.SemaphoreType.DMA
    anyspace = pl.BlockSpec(memory_space=pl.ANY)
    shapes = (
        jax.ShapeDtypeStruct((ROWS, WIDE), BF16),
        jax.ShapeDtypeStruct((PIECE, FULL), BF16),
        jax.ShapeDtypeStruct((PIECE, FULL), BF16),
        jax.ShapeDtypeStruct((OWN, WIDE), BF16),
    )
    results = pl.pallas_call(
        kernel,
        out_shape=shapes,
        in_specs=[anyspace] * 5,
        out_specs=(anyspace,) * 4,
        scratch_shapes=[
            vm((2, STEPS, 2, 2, ROWS, WIDE), BF16),
            vm((DEEP, PIECE, 1024), BF16),
            vm((2, WIDE, WIN), BF16),
            vm((WIDE, 2 * PAD), BF16),
            vm((2 * PAD, WIDE), BF16),
            vm((PAD, WIDE), BF16),
            vm((DEEP, 2, ROWS, SUMS), F32),
            vm((STEPS, ROWS, SUMS), F32),
            vm((DEEP, STEPS, ROWS, SUMS), BF16),
            vm((3, STEPS, ROWS, SUMS), BF16),
            vm((2, STEPS, HALF, SUMS), F32),
            vm((STEPS, HALF, SUMS), F32),
            vm((CHUNKS, STEPS, 4, 2, HALF, LANES), BF16),
            vm((GU, DEEP, PIECE, LANES), BF16),
            vm((GU, DEEP, PIECE, LANES), BF16),
            vm((PIECE, FULL), BF16),
            vm((PIECE, FULL), BF16),
            vm((PAD, WIDE), BF16),
            vm((2, 2, STEPS, ROWS, WIDE), F32),
            vm((2, STEPS, ROWS, WIDE), F32),
            vm((ROWS, WIDE), BF16),
            vm((ROWS, WIDE), BF16),
            vm((STEPS, 2, ROWS, WIDE), BF16),
            vm((STEPS, 2, ROWS, WIDE), BF16),
            vm((2, ROWS, WIDE), F32),
            vm((ROWS, WIDE), BF16),
            dma((5,)),
            dma((9,)), dma((9,)),
            dma((9,)), dma((9,)),
            dma((8,)), dma((8,)),
            dma((8,)), dma((8,)),
            dma, dma,
            dma((5, 3)), dma((5, 3)),
            dma((5,)), dma((5,)),
            dma((5,)), dma((5,)),
            dma((10, 2)), dma((10, 2)),
            dma((10, 2)), dma((10, 2)),
            dma((GU, 4)), dma((GU, 4)),
            dma((5,)), dma((5,)),
            dma, dma,
            dma((8,)), dma((8,)),
            dma((4,)),
        ],
        compiler_params=pltpu.CompilerParams(
            collective_id=0, has_side_effects=True, vmem_limit_bytes=60 * 1024 * 1024
        ),
        cost_estimate=pl.CostEstimate(flops=8 * 10**9, bytes_accessed=12 * 10**6, transcendentals=10**6),
        name="ffn_backward",
    )(inputs, out_grad, w_gate, w_up, w_down)
    return pl.pallas_call(
        hand_on,
        out_shape=shapes,
        in_specs=[pl.BlockSpec(memory_space=pltpu.VMEM)] * 4,
        out_specs=(anyspace,) * 4,
        scratch_shapes=[dma((4,))],
        name="hand_on",
    )(*results)


def solution(mesh):
    placed = (
        P(("depth", "col"), "row"),
        P(("depth", "col"), "row"),
        P("row", "col"),
        P("row", "col"),
        P("col", "row"),
    )
    return jax.shard_map(
        on_device,
        mesh=mesh,
        in_specs=placed,
        out_specs=(
            P(("depth", "col"), "row"),
            P(("row", "depth"), "col"),
            P(("row", "depth"), "col"),
            P(("col", "depth"), "row"),
        ),
        check_vma=False,
    )
```

```python
import jax
import jax.numpy as jnp
from jax import lax
from jax.experimental import pallas as pl
from jax.experimental.pallas import tpu as pltpu
from jax.sharding import PartitionSpec as P

MESH = pl.DeviceIdType.MESH
F32, BF16 = jnp.float32, jnp.bfloat16

DELTA = (0, 1, -1, 2, -2, 3, -3, 4)
DEEP = 4
STEPS = 8
ROWS = 32
WIDE = 896
FULL = 1920
OWN = 480
PAD = 512
WIN = 640
PIECE = 224
HALF = ROWS // 2
CUT = 128
GU = 4
CHUNKS = 6
LANES = 2 * CUT
SUMS = 3 * PAD
GROUPS = ((0, 1), (1, 3), (3, 5), (5, 7), (7, 8))
PARTS = tuple((k, 0, 5) for k in range(4)) + tuple((k, 5, 8) for k in range(4)) + ((4, 0, 8), (5, 0, 8))


def mm(a, b):
    return lax.dot_general(a, b, (((1,), (0,)), ((), ())), preferred_element_type=F32)


def mm_t(a, b):
    return lax.dot_general(a, b, (((1,), (1,)), ((), ())), preferred_element_type=F32)


def kernel(
    x_hbm, dy_hbm, wg_hbm, wu_hbm, wd_hbm,
    ig_out, gate_out, up_out, down_out,
    xd, xt, win, w2, w2t, wd, part, part_own, psend, precv, ysum, xrecv, g,
    piece_send, piece_recv, gate_fin, up_fin, down, ig, ig_core, ig_xs, ig_xr, ig_zs, ig_zr, ig_fin, ig_res,
    load_sem, zo_s, zo_r, zf_s, zf_r, co_s, co_r, cf_s, cf_r, x0_s, x0_r, y_s, y_r, h_s, h_r,
    ah_s, ah_r, ay_s, ay_r, af_s, af_r, p_s, p_r, ic_s, ic_r, ix_s, ix_r, iz_s, iz_r, out_sem,
):
    row, z, dep = lax.axis_index("row"), lax.axis_index("col"), lax.axis_index("depth")
    y, xh = row // 2, row % 2
    xl, c = dep // 2, dep % 2
    dep_x = (1 - xl) * 2 + c
    dep_c = xl * 2 + 1 - c
    dep_xc = (1 - xl) * 2 + 1 - c
    y_up, y_down = (y + 1) % 4, (y + 3) % 4

    def at_row(yy, hh):
        return {"row": yy * 2 + hh, "col": z, "depth": dep}

    def at_depth(d):
        return {"row": row, "col": z, "depth": d}

    def at_col(zz):
        return {"row": row, "col": zz, "depth": dep}

    x_peer = at_row(y, 1 - xh)

    def remote(src, dst, ss, rs, dev):
        return pltpu.make_async_remote_copy(
            src_ref=src, dst_ref=dst, send_sem=ss, recv_sem=rs, device_id=dev, device_id_type=MESH
        )

    start = jnp.where(dep == 3, 1280, dep * 480 - (dep * 480) % 128)
    start = pl.multiple_of(start, 128)
    shift = dep * 480 - start
    loads = [
        pltpu.make_async_copy(x_hbm, xd.at[0, 0, xl, c], load_sem.at[0]),
        pltpu.make_async_copy(dy_hbm, xd.at[1, 0, xl, c], load_sem.at[1]),
        pltpu.make_async_copy(wg_hbm.at[:, pl.ds(start, WIN)], win.at[0], load_sem.at[2]),
        pltpu.make_async_copy(wu_hbm.at[:, pl.ds(start, WIN)], win.at[1], load_sem.at[3]),
        pltpu.make_async_copy(wd_hbm.at[pl.ds(dep * OWN, OWN)], wd.at[pl.ds(0, OWN)], load_sem.at[4]),
    ]
    for cp in loads:
        cp.start()

    barrier = pltpu.get_barrier_semaphore()
    peers = [at_depth(dep_x), at_depth(dep_c), at_depth(dep_xc)]
    peers += [at_col((z + m) % STEPS) for m in range(1, STEPS)]
    peers += [at_row((y + m) % 4, xh) for m in (1, 2, 3)] + [x_peer]
    peers += [{"row": row, "col": (z + m) % STEPS, "depth": dep_x} for m in (1, STEPS - 1)]
    for dev in peers:
        pl.semaphore_signal(barrier, inc=1, device_id=dev, device_id_type=MESH)

    pick = (
        lax.broadcasted_iota(jnp.int32, (WIN, PAD), 0) - lax.broadcasted_iota(jnp.int32, (WIN, PAD), 1) == shift
    ) & (lax.broadcasted_iota(jnp.int32, (WIN, PAD), 1) < OWN)
    pick = jnp.where(pick, 1.0, 0.0).astype(BF16)

    def select(i):
        loads[2 + i].wait()

        def one(t, carry):
            r = pl.ds(pl.multiple_of(t * 224, 32), 224)
            cut = mm(win[i, r], pick).astype(BF16)
            for k in range(GU):
                w2[r, k * LANES + i * CUT : k * LANES + (i + 1) * CUT] = cut[:, k * CUT : (k + 1) * CUT]
            return carry

        lax.fori_loop(0, 4, one, 0)

    select(0)
    loads[0].wait()
    loads[1].wait()
    pl.semaphore_wait(barrier, len(peers))

    def block(s, a, b):
        return xd.at[:, s, a, b]

    def ring(s, a, ss, rs):
        to = (z + STEPS - 1) % STEPS if s % 2 else (z + 1) % STEPS
        return remote(block(max(s - 2, 0), a, c), block(s, a, c), ss.at[s], rs.at[s], at_col(to))

    def ring_last(a, ss, rs, i):
        to = (z + 1) % STEPS if i == 0 else (z + STEPS - 1) % STEPS
        src = 6 if i == 0 else 5
        return remote(xd.at[i, src, a, c], xd.at[i, 7, a, c], ss.at[7 + i], rs.at[7 + i], at_col(to))

    def to_core(s, a, ss, rs):
        return remote(block(s, a, c), block(s, a, c), ss.at[s], rs.at[s], at_depth(dep_c))

    def to_x():
        return remote(block(0, xl, c), block(0, xl, c), x0_s, x0_r, at_depth(dep_x))

    def diagonal(s):
        to = (z + STEPS - 1) % STEPS if s == 1 else (z + 1) % STEPS
        dev = {"row": row, "col": to, "depth": dep_x}
        return remote(block(0, xl, c), block(s, xl, c), zf_s.at[s], zf_r.at[s], dev)

    to_x().start()
    ring(1, xl, zo_s, zo_r).start()
    ring(2, xl, zo_s, zo_r).start()
    diagonal(1).start()
    diagonal(2).start()
    to_core(0, xl, co_s, co_r).start()

    select(1)
    loads[4].wait()
    wd[OWN:PAD, :] = jnp.zeros((PAD - OWN, WIDE), BF16)

    def arrive_pair(m, a, zs, zr, cs, cr):
        for s in (2 * m - 1, 2 * m):
            ring(s, a, zs, zr).wait_recv()
            if m < 3:
                ring(s + 2, a, zs, zr).start()
            else:
                ring_last(a, zs, zr, s % 2).start()
        for s in (2 * m - 1, 2 * m):
            to_core(s, a, cs, cr).start()

    def arrive_last(a, zs, zr, cs, cr):
        ring_last(a, zs, zr, 0).wait_recv()
        ring_last(a, zs, zr, 1).wait_recv()
        to_core(7, a, cs, cr).start()

    own_sems = (zo_s, zo_r, co_s, co_r)
    far_sems = (zf_s, zf_r, cf_s, cf_r)

    def y_send(q, j):
        d = (y + 4 - j) % 4
        rows = pl.ds(GROUPS[q][0], GROUPS[q][1] - GROUPS[q][0])
        return remote(psend.at[d, rows], precv.at[j - 1, rows], y_s.at[q, j - 1], y_r.at[q, j - 1], at_row(d, xh))

    def x_send(q):
        rows = pl.ds(GROUPS[q][0], GROUPS[q][1] - GROUPS[q][0])
        return remote(ysum.at[1 - xh, rows], xrecv.at[rows], h_s.at[q], h_r.at[q], x_peer)

    def ag_x(q):
        lo, hi = GROUPS[q]
        rows = g.at[:, lo:hi, y, xh]
        return remote(rows, rows, ah_s.at[q], ah_r.at[q], x_peer)

    def ag_x_wait(q):
        lo, hi = GROUPS[q]
        rows = g.at[:, lo:hi, y, 1 - xh]
        remote(rows, rows, ah_s.at[q], ah_r.at[q], x_peer).wait_recv()

    def stage_products(q):
        lo, hi = GROUPS[q]
        n = hi - lo
        for s in range(lo, hi):
            to_core(s, xl, co_s, co_r).wait_recv()
            to_core(s, 1 - xl, cf_s, cf_r).wait_recv()
        xs = xd[0, lo:hi].reshape(n * 128, WIDE)
        ds = xd[1, lo:hi].reshape(n * 128, WIDE)
        for a, b, p in ((0, 2 * PAD, mm(xs, w2[...])), (2 * PAD, SUMS, mm_t(ds, wd[...]))):
            p = p.reshape(n, DEEP, ROWS, b - a)
            for s in range(n):
                part[:, s, :, a:b] = p[s]
                psend[:, lo + s, :, a:b] = p[s].astype(BF16)
        for j in (2, 1, 3):
            y_send(q, j).start()
        part_own[lo:hi] = part[y, 0:n]
        for s in range(lo, hi):
            xt[:, :, s * 128 : (s + 1) * 128] = xd[0, s].reshape(128, WIDE).T.reshape(DEEP, PIECE, 128)

    def stage_y(q):
        lo, hi = GROUPS[q]
        for j in (1, 3, 2):
            y_send(q, j).wait_recv()
        for s in range(lo, hi):
            total = part_own[s]
            for j in (1, 3, 2):
                total = total + precv[j - 1, s].astype(F32)
            total = total.reshape(2, HALF, SUMS)
            ysum[0, s] = total[0]
            ysum[1, s] = total[1]
        x_send(q).start()

    def stage_x(q):
        lo, hi = GROUPS[q]
        x_send(q).wait_recv()
        for s in range(lo, hi):
            total = ysum[xh, s] + xrecv[s]
            for k in range(GU):
                gate = total[:, k * LANES : k * LANES + CUT]
                up = total[:, k * LANES + CUT : (k + 1) * LANES]
                back = total[:, 2 * PAD + k * CUT : 2 * PAD + (k + 1) * CUT]
                sigma = jax.nn.sigmoid(gate)
                lanes = slice((k % 2) * CUT, (k % 2 + 1) * CUT)
                g[GU + k // 2, s, y, xh, :, lanes] = (gate * sigma * up).astype(BF16)
                g[k, s, y, xh, :, 0:CUT] = (back * up * sigma * (1.0 + gate * (1.0 - sigma))).astype(BF16)
                g[k, s, y, xh, :, CUT:LANES] = (back * gate * sigma).astype(BF16)
        ag_x(q).start()

    def ag_own(p, up):
        k, lo, hi = PARTS[p]
        rows = g.at[k, lo:hi, y]
        i = 0 if up else 1
        return remote(rows, rows, ay_s.at[p, i], ay_r.at[p, i], at_row(y_up if up else y_down, xh))

    def ag_own_wait(p, up):
        k, lo, hi = PARTS[p]
        rows = g.at[k, lo:hi, y_down if up else y_up]
        i = 0 if up else 1
        remote(rows, rows, ay_s.at[p, i], ay_r.at[p, i], at_row(y_up, xh)).wait_recv()

    def ag_pass(p, up):
        k, lo, hi = PARTS[p]
        i = 0 if up else 1
        rows = g.at[k, lo:hi, y_down if up else y_up, i]
        return remote(rows, rows, af_s.at[p, i], af_r.at[p, i], at_row(y_up if up else y_down, xh))

    def ag_pass_wait(p, up):
        k, lo, hi = PARTS[p]
        i = 0 if up else 1
        rows = g.at[k, lo:hi, (y + 2) % 4, i]
        remote(rows, rows, af_s.at[p, i], af_r.at[p, i], at_row(y_up, xh)).wait_recv()

    def ag_start(p):
        for up in (True, False):
            ag_own(p, up).start()

    def ag_middle(p):
        for up in (True, False):
            ag_own_wait(p, up)
            ag_pass(p, up).start()

    def ag_end(p):
        for up in (True, False):
            ag_pass_wait(p, up)

    src = block(0, 1 - xl, c)
    remote(src, src, x0_s, x0_r, at_depth(dep_x)).wait_recv()
    to_core(0, 1 - xl, cf_s, cf_r).start()
    arrive_pair(1, xl, *own_sems)
    stage_products(0)
    arrive_pair(1, 1 - xl, *far_sems)
    arrive_pair(2, xl, *own_sems)
    stage_products(1)
    arrive_pair(2, 1 - xl, *far_sems)
    arrive_pair(3, xl, *own_sems)
    stage_y(0)
    stage_products(2)
    arrive_pair(3, 1 - xl, *far_sems)
    arrive_last(xl, *own_sems)
    stage_x(0)
    stage_products(3)
    stage_y(1)
    arrive_last(1 - xl, *far_sems)
    stage_products(4)
    stage_x(1)
    stage_y(2)
    for k in range(GU):
        w2t[k * LANES : (k + 1) * LANES, :] = w2[:, k * LANES : (k + 1) * LANES].T
    stage_x(2)
    stage_y(3)
    for q in range(3):
        ag_x_wait(q)
    for p in range(4):
        ag_start(p)
    stage_x(3)
    stage_y(4)
    stage_x(4)
    for p in range(4):
        ag_middle(p)
    for q in (3, 4):
        ag_x_wait(q)

    def piece(k, j):
        d = (dep + j) % DEEP
        return remote(piece_send.at[k, d], piece_recv.at[k, dep], p_s.at[k, j], p_r.at[k, j], at_depth(d))

    def piece_wait(k, j):
        dst = piece_recv.at[k, (dep + DEEP - j) % DEEP]
        remote(dst, dst, p_s.at[k, j], p_r.at[k, j], at_depth(dep_x)).wait_recv()

    def pieces(k):
        gk = g[k].reshape(1024, LANES)
        piece_send[k] = mm(xt[...].reshape(WIDE, 1024), gk).astype(BF16).reshape(DEEP, PIECE, LANES)

    def pieces_start(k):
        for j in (2, 1, 3):
            piece(k, j).start()
        piece_recv[k, dep] = piece_send[k, dep]

    def ig_group(q):
        lo, hi = GROUPS[q]
        r = 0.0
        for k in range(GU):
            r = r + mm(g[k, lo:hi].reshape((hi - lo) * 128, LANES), w2t[k * LANES : (k + 1) * LANES, :])
        r = r.reshape(hi - lo, 2, 2, ROWS, WIDE)
        for s in range(lo, hi):
            for a in range(2):
                for b in range(2):
                    ig[b, a, s] = r[s - lo, a, b]
        ig_c(q).start()

    def ig_c(q):
        lo, hi = GROUPS[q]
        return remote(ig.at[1 - c, :, lo:hi], ig_core.at[:, lo:hi], ic_s.at[q], ic_r.at[q], at_depth(dep_c))

    def ig_z(s):
        return remote(ig_zs.at[s], ig_zr.at[s], iz_s.at[s], iz_r.at[s], at_col((z + DELTA[s] + STEPS) % STEPS))

    def ig_chip(q):
        lo, hi = GROUPS[q]
        ig_c(q).wait_recv()
        for s in range(lo, hi):
            total = ig[c, :, s] + ig_core[:, s]
            if s:
                ig_zs[s] = total.astype(BF16)
                ig_z(s).start()
            else:
                ig_fin[...] = total

    for p in range(4, 8):
        ag_start(p)
    for p in range(4):
        ag_end(p)
    ig_group(2)
    ag_middle(4)
    ag_middle(5)
    ig_group(1)
    ag_middle(6)
    ag_middle(7)
    ag_start(8)
    ag_start(9)
    ag_end(4)
    pieces(0)
    pieces_start(0)
    ig_chip(2)
    ig_group(0)
    ag_end(5)
    pieces(1)
    pieces_start(1)
    ig_chip(1)
    ig_chip(0)
    ag_end(6)
    ag_end(7)
    ig_group(4)
    ig_group(3)
    pieces(2)
    pieces_start(2)
    ig_chip(4)
    ig_chip(3)
    pieces(3)
    pieces_start(3)
    ag_middle(8)
    ag_middle(9)

    ag_end(8)
    ag_end(9)

    def down_step(t, carry):
        h = g[GU + t].reshape(1024, LANES)
        r = lax.dot_general(h, xd[1].reshape(1024, WIDE), (((0,), (0,)), ((), ())), preferred_element_type=F32)
        down[pl.ds(pl.multiple_of(t * LANES, LANES), LANES), :] = r.astype(BF16)
        return carry

    lax.fori_loop(0, 2, down_step, 0)
    outs = [pltpu.make_async_copy(down.at[pl.ds(0, OWN)], down_out, out_sem.at[0])]
    outs[0].start()

    def assemble(k):
        for j in (1, 2, 3):
            piece_wait(k, j)
        wide = min(CUT, OWN - k * CUT)
        for src in range(DEEP):
            lanes = slice(src * OWN + k * CUT, src * OWN + k * CUT + wide)
            gate_fin[:, lanes] = piece_recv[k, src, :, 0:wide]
            up_fin[:, lanes] = piece_recv[k, src, :, CUT : CUT + wide]

    assemble(0)
    assemble(1)
    total = ig_fin[...]
    for s in range(1, STEPS):
        ig_z(s).wait_recv()
        total = total + ig_zr[s].astype(F32)
    ig_fin[...] = total

    ig_xs[...] = ig_fin[1 - xl].astype(BF16)
    ig_x = remote(ig_xs, ig_xr, ix_s, ix_r, at_depth(dep_x))
    ig_x.start()
    assemble(2)
    ig_x.wait_recv()
    ig_res[...] = (ig_fin[xl] + ig_xr[...].astype(F32)).astype(BF16)
    outs.append(pltpu.make_async_copy(ig_res, ig_out, out_sem.at[3]))
    outs[-1].start()
    assemble(3)
    for i, (src, dst) in enumerate(((gate_fin, gate_out), (up_fin, up_out))):
        outs.append(pltpu.make_async_copy(src, dst, out_sem.at[1 + i]))
        outs[-1].start()

    to_x().wait_send()
    diagonal(1).wait_send()
    diagonal(2).wait_send()
    for a, zs, zr, cs, cr in ((xl, *own_sems), (1 - xl, *far_sems)):
        ring_last(a, zs, zr, 0).wait_send()
        ring_last(a, zs, zr, 1).wait_send()

        for s in range(1 if zs is zo_s else 3, 7):
            ring(s, a, zs, zr).wait_send()
        for s in range(STEPS):
            to_core(s, a, cs, cr).wait_send()

    for q in range(len(GROUPS)):
        for j in (1, 2, 3):
            y_send(q, j).wait_send()
        x_send(q).wait_send()
        ag_x(q).wait_send()
    for p in range(len(PARTS)):
        for up in (True, False):
            ag_own(p, up).wait_send()
            ag_pass(p, up).wait_send()
    for k in range(GU):
        for j in (1, 2, 3):
            piece(k, j).wait_send()
    for q in range(len(GROUPS)):
        ig_c(q).wait_send()
    ig_x.wait_send()
    for s in range(1, STEPS):
        ig_z(s).wait_send()
    for cp in outs:
        cp.wait()


def hand_on(a0, a1, a2, a3, b0, b1, b2, b3, v0, v1, v2, v3, sem_in, sem_out):
    sets = ((a1, v1, b1), (a2, v2, b2), (a3, v3, b3), (a0, v0, b0))
    loads = [pltpu.make_async_copy(a, v, sem_in.at[i]) for i, (a, v, b) in enumerate(sets)]
    stores = [pltpu.make_async_copy(v, b, sem_out.at[i]) for i, (a, v, b) in enumerate(sets)]
    for cp in loads:
        cp.start()
    for load, store in zip(loads, stores):
        load.wait()
        store.start()
    for cp in stores:
        cp.wait()


def on_device(inputs, out_grad, w_gate, w_up, w_down):
    vm = pltpu.VMEM
    dma = pltpu.SemaphoreType.DMA
    anyspace = pl.BlockSpec(memory_space=pl.ANY)
    shapes = (
        jax.ShapeDtypeStruct((ROWS, WIDE), BF16),
        jax.ShapeDtypeStruct((PIECE, FULL), BF16),
        jax.ShapeDtypeStruct((PIECE, FULL), BF16),
        jax.ShapeDtypeStruct((OWN, WIDE), BF16),
    )
    results = pl.pallas_call(
        kernel,
        out_shape=shapes,
        in_specs=[anyspace] * 5,
        out_specs=(anyspace,) * 4,
        scratch_shapes=[
            vm((2, STEPS, 2, 2, ROWS, WIDE), BF16),
            vm((DEEP, PIECE, 1024), BF16),
            vm((2, WIDE, WIN), BF16),
            vm((WIDE, 2 * PAD), BF16),
            vm((2 * PAD, WIDE), BF16),
            vm((PAD, WIDE), BF16),
            vm((DEEP, 2, ROWS, SUMS), F32),
            vm((STEPS, ROWS, SUMS), F32),
            vm((DEEP, STEPS, ROWS, SUMS), BF16),
            vm((3, STEPS, ROWS, SUMS), BF16),
            vm((2, STEPS, HALF, SUMS), F32),
            vm((STEPS, HALF, SUMS), F32),
            vm((CHUNKS, STEPS, 4, 2, HALF, LANES), BF16),
            vm((GU, DEEP, PIECE, LANES), BF16),
            vm((GU, DEEP, PIECE, LANES), BF16),
            vm((PIECE, FULL), BF16),
            vm((PIECE, FULL), BF16),
            vm((PAD, WIDE), BF16),
            vm((2, 2, STEPS, ROWS, WIDE), F32),
            vm((2, STEPS, ROWS, WIDE), F32),
            vm((ROWS, WIDE), BF16),
            vm((ROWS, WIDE), BF16),
            vm((STEPS, 2, ROWS, WIDE), BF16),
            vm((STEPS, 2, ROWS, WIDE), BF16),
            vm((2, ROWS, WIDE), F32),
            vm((ROWS, WIDE), BF16),
            dma((5,)),
            dma((9,)), dma((9,)),
            dma((9,)), dma((9,)),
            dma((8,)), dma((8,)),
            dma((8,)), dma((8,)),
            dma, dma,
            dma((5, 3)), dma((5, 3)),
            dma((5,)), dma((5,)),
            dma((5,)), dma((5,)),
            dma((10, 2)), dma((10, 2)),
            dma((10, 2)), dma((10, 2)),
            dma((GU, 4)), dma((GU, 4)),
            dma((5,)), dma((5,)),
            dma, dma,
            dma((8,)), dma((8,)),
            dma((4,)),
        ],
        compiler_params=pltpu.CompilerParams(
            collective_id=0, has_side_effects=True, vmem_limit_bytes=60 * 1024 * 1024
        ),
        cost_estimate=pl.CostEstimate(flops=8 * 10**9, bytes_accessed=12 * 10**6, transcendentals=10**6),
        name="ffn_backward",
    )(inputs, out_grad, w_gate, w_up, w_down)
    return pl.pallas_call(
        hand_on,
        out_shape=shapes,
        in_specs=[anyspace] * 4,
        out_specs=(anyspace,) * 4,
        scratch_shapes=[vm(a.shape, BF16) for a in shapes] + [dma((4,)), dma((4,))],
        name="hand_on",
    )(*results)


def solution(mesh):
    placed = (
        P(("depth", "col"), "row"),
        P(("depth", "col"), "row"),
        P("row", "col"),
        P("row", "col"),
        P("col", "row"),
    )
    return jax.shard_map(
        on_device,
        mesh=mesh,
        in_specs=placed,
        out_specs=(
            P(("depth", "col"), "row"),
            P(("row", "depth"), "col"),
            P(("row", "depth"), "col"),
            P(("col", "depth"), "row"),
        ),
        check_vma=False,
    )
```

```python
import jax
import jax.numpy as jnp
from jax import lax
from jax.experimental import pallas as pl
from jax.experimental.pallas import tpu as pltpu
from jax.sharding import PartitionSpec as P

MESH = pl.DeviceIdType.MESH
F32, BF16 = jnp.float32, jnp.bfloat16

DELTA = (0, 1, -1, 2, -2, 3, -3, 4)
DEEP = 4
STEPS = 8
ROWS = 32
WIDE = 896
FULL = 1920
OWN = 480
PAD = 512
WIN = 640
PIECE = 224
HALF = ROWS // 2
CUT = 128
GU = 4
CHUNKS = 6
LANES = 2 * CUT
SUMS = 3 * PAD
GROUPS = ((0, 1), (1, 3), (3, 5), (5, 7), (7, 8))
PARTS = tuple((k, 0, 5) for k in range(4)) + tuple((k, 5, 8) for k in range(4)) + ((4, 0, 8), (5, 0, 8))


def mm(a, b):
    return lax.dot_general(a, b, (((1,), (0,)), ((), ())), preferred_element_type=F32)


def mm_t(a, b):
    return lax.dot_general(a, b, (((1,), (1,)), ((), ())), preferred_element_type=F32)


def kernel(
    x_hbm, dy_hbm, wg_hbm, wu_hbm, wd_hbm,
    ig_out, gate_out, up_out, down_out,
    xd, xt, win, w2, w2t, wd, part, part_own, psend, precv, ysum, xrecv, g,
    piece_send, piece_recv, gate_fin, up_fin, down, ig, ig_core, ig_xs, ig_xr, ig_zs, ig_zr, ig_fin, ig_res,
    load_sem, zo_s, zo_r, zf_s, zf_r, co_s, co_r, cf_s, cf_r, x0_s, x0_r, y_s, y_r, h_s, h_r,
    ah_s, ah_r, ay_s, ay_r, af_s, af_r, p_s, p_r, ic_s, ic_r, ix_s, ix_r, iz_s, iz_r, out_sem,
):
    row, z, dep = lax.axis_index("row"), lax.axis_index("col"), lax.axis_index("depth")
    y, xh = row // 2, row % 2
    xl, c = dep // 2, dep % 2
    dep_x = (1 - xl) * 2 + c
    dep_c = xl * 2 + 1 - c
    dep_xc = (1 - xl) * 2 + 1 - c
    y_up, y_down = (y + 1) % 4, (y + 3) % 4

    def at_row(yy, hh):
        return {"row": yy * 2 + hh, "col": z, "depth": dep}

    def at_depth(d):
        return {"row": row, "col": z, "depth": d}

    def at_col(zz):
        return {"row": row, "col": zz, "depth": dep}

    x_peer = at_row(y, 1 - xh)

    def remote(src, dst, ss, rs, dev):
        return pltpu.make_async_remote_copy(
            src_ref=src, dst_ref=dst, send_sem=ss, recv_sem=rs, device_id=dev, device_id_type=MESH
        )

    start = jnp.where(dep == 3, 1280, dep * 480 - (dep * 480) % 128)
    start = pl.multiple_of(start, 128)
    shift = dep * 480 - start
    loads = [
        pltpu.make_async_copy(x_hbm, xd.at[0, 0, xl, c], load_sem.at[0]),
        pltpu.make_async_copy(dy_hbm, xd.at[1, 0, xl, c], load_sem.at[1]),
        pltpu.make_async_copy(wg_hbm.at[:, pl.ds(start, WIN)], win.at[0], load_sem.at[2]),
        pltpu.make_async_copy(wu_hbm.at[:, pl.ds(start, WIN)], win.at[1], load_sem.at[3]),
        pltpu.make_async_copy(wd_hbm.at[pl.ds(dep * OWN, OWN)], wd.at[pl.ds(0, OWN)], load_sem.at[4]),
    ]
    for cp in loads:
        cp.start()

    barrier = pltpu.get_barrier_semaphore()
    peers = [at_depth(dep_x), at_depth(dep_c), at_depth(dep_xc)]
    peers += [at_col((z + m) % STEPS) for m in range(1, STEPS)]
    peers += [at_row((y + m) % 4, xh) for m in (1, 2, 3)] + [x_peer]
    peers += [{"row": row, "col": (z + m) % STEPS, "depth": dep_x} for m in (1, STEPS - 1)]
    for dev in peers:
        pl.semaphore_signal(barrier, inc=1, device_id=dev, device_id_type=MESH)

    pick = (
        lax.broadcasted_iota(jnp.int32, (WIN, PAD), 0) - lax.broadcasted_iota(jnp.int32, (WIN, PAD), 1) == shift
    ) & (lax.broadcasted_iota(jnp.int32, (WIN, PAD), 1) < OWN)
    pick = jnp.where(pick, 1.0, 0.0).astype(BF16)

    def select(i):
        loads[2 + i].wait()

        def one(t, carry):
            r = pl.ds(pl.multiple_of(t * 224, 32), 224)
            cut = mm(win[i, r], pick).astype(BF16)
            for k in range(GU):
                w2[r, k * LANES + i * CUT : k * LANES + (i + 1) * CUT] = cut[:, k * CUT : (k + 1) * CUT]
            return carry

        lax.fori_loop(0, 4, one, 0)

    loads[0].wait()
    loads[1].wait()
    pl.semaphore_wait(barrier, len(peers))

    def block(s, a, b):
        return xd.at[:, s, a, b]

    def ring(s, a, ss, rs):
        to = (z + STEPS - 1) % STEPS if s % 2 else (z + 1) % STEPS
        return remote(block(max(s - 2, 0), a, c), block(s, a, c), ss.at[s], rs.at[s], at_col(to))

    def ring_last(a, ss, rs, i):
        to = (z + 1) % STEPS if i == 0 else (z + STEPS - 1) % STEPS
        src = 6 if i == 0 else 5
        return remote(xd.at[i, src, a, c], xd.at[i, 7, a, c], ss.at[7 + i], rs.at[7 + i], at_col(to))

    def to_core(s, a, ss, rs):
        return remote(block(s, a, c), block(s, a, c), ss.at[s], rs.at[s], at_depth(dep_c))

    def to_x():
        return remote(block(0, xl, c), block(0, xl, c), x0_s, x0_r, at_depth(dep_x))

    def diagonal(s):
        to = (z + STEPS - 1) % STEPS if s == 1 else (z + 1) % STEPS
        dev = {"row": row, "col": to, "depth": dep_x}
        return remote(block(0, xl, c), block(s, xl, c), zf_s.at[s], zf_r.at[s], dev)

    to_x().start()
    ring(1, xl, zo_s, zo_r).start()
    ring(2, xl, zo_s, zo_r).start()
    diagonal(1).start()
    diagonal(2).start()
    to_core(0, xl, co_s, co_r).start()

    select(0)
    select(1)
    loads[4].wait()
    wd[OWN:PAD, :] = jnp.zeros((PAD - OWN, WIDE), BF16)

    def arrive_pair(m, a, zs, zr, cs, cr):
        for s in (2 * m - 1, 2 * m):
            ring(s, a, zs, zr).wait_recv()
            if m < 3:
                ring(s + 2, a, zs, zr).start()
            else:
                ring_last(a, zs, zr, s % 2).start()
        for s in (2 * m - 1, 2 * m):
            to_core(s, a, cs, cr).start()

    def arrive_last(a, zs, zr, cs, cr):
        ring_last(a, zs, zr, 0).wait_recv()
        ring_last(a, zs, zr, 1).wait_recv()
        to_core(7, a, cs, cr).start()

    own_sems = (zo_s, zo_r, co_s, co_r)
    far_sems = (zf_s, zf_r, cf_s, cf_r)

    def y_send(q, j):
        d = (y + 4 - j) % 4
        rows = pl.ds(GROUPS[q][0], GROUPS[q][1] - GROUPS[q][0])
        return remote(psend.at[d, rows], precv.at[j - 1, rows], y_s.at[q, j - 1], y_r.at[q, j - 1], at_row(d, xh))

    def x_send(q):
        rows = pl.ds(GROUPS[q][0], GROUPS[q][1] - GROUPS[q][0])
        return remote(ysum.at[1 - xh, rows], xrecv.at[rows], h_s.at[q], h_r.at[q], x_peer)

    def ag_x(q):
        lo, hi = GROUPS[q]
        rows = g.at[0:GU, lo:hi, y, xh]
        return remote(rows, rows, ah_s.at[q], ah_r.at[q], x_peer)

    def ag_x_wait(q):
        lo, hi = GROUPS[q]
        rows = g.at[0:GU, lo:hi, y, 1 - xh]
        remote(rows, rows, ah_s.at[q], ah_r.at[q], x_peer).wait_recv()

    def ag_x_hidden(half):
        rows = g.at[GU:CHUNKS, :, y, half]
        return remote(rows, rows, ah_s.at[5], ah_r.at[5], x_peer)

    def stage_products(q):
        lo, hi = GROUPS[q]
        n = hi - lo
        for s in range(lo, hi):
            to_core(s, xl, co_s, co_r).wait_recv()
            to_core(s, 1 - xl, cf_s, cf_r).wait_recv()
        xs = xd[0, lo:hi].reshape(n * 128, WIDE)
        ds = xd[1, lo:hi].reshape(n * 128, WIDE)
        for a, b, p in ((0, 2 * PAD, mm(xs, w2[...])), (2 * PAD, SUMS, mm_t(ds, wd[...]))):
            p = p.reshape(n, DEEP, ROWS, b - a)
            for s in range(n):
                part[:, s, :, a:b] = p[s]
                psend[:, lo + s, :, a:b] = p[s].astype(BF16)
        for j in (2, 1, 3):
            y_send(q, j).start()
        part_own[lo:hi] = part[y, 0:n]
        for s in range(lo, hi):
            xt[:, :, s * 128 : (s + 1) * 128] = xd[0, s].reshape(128, WIDE).T.reshape(DEEP, PIECE, 128)

    def stage_y(q):
        lo, hi = GROUPS[q]
        for j in (1, 3, 2):
            y_send(q, j).wait_recv()
        for s in range(lo, hi):
            total = part_own[s]
            for j in (1, 3, 2):
                total = total + precv[j - 1, s].astype(F32)
            total = total.reshape(2, HALF, SUMS)
            ysum[0, s] = total[0]
            ysum[1, s] = total[1]
        x_send(q).start()

    def stage_x(q):
        lo, hi = GROUPS[q]
        x_send(q).wait_recv()
        for s in range(lo, hi):
            total = ysum[xh, s] + xrecv[s]
            for k in range(GU):
                gate = total[:, k * LANES : k * LANES + CUT]
                up = total[:, k * LANES + CUT : (k + 1) * LANES]
                back = total[:, 2 * PAD + k * CUT : 2 * PAD + (k + 1) * CUT]
                sigma = jax.nn.sigmoid(gate)
                lanes = slice((k % 2) * CUT, (k % 2 + 1) * CUT)
                g[GU + k // 2, s, y, xh, :, lanes] = (gate * sigma * up).astype(BF16)
                g[k, s, y, xh, :, 0:CUT] = (back * up * sigma * (1.0 + gate * (1.0 - sigma))).astype(BF16)
                g[k, s, y, xh, :, CUT:LANES] = (back * gate * sigma).astype(BF16)
        ag_x(q).start()

    def ag_own(p, up):
        k, lo, hi = PARTS[p]
        rows = g.at[k, lo:hi, y]
        i = 0 if up else 1
        return remote(rows, rows, ay_s.at[p, i], ay_r.at[p, i], at_row(y_up if up else y_down, xh))

    def ag_own_wait(p, up):
        k, lo, hi = PARTS[p]
        rows = g.at[k, lo:hi, y_down if up else y_up]
        i = 0 if up else 1
        remote(rows, rows, ay_s.at[p, i], ay_r.at[p, i], at_row(y_up, xh)).wait_recv()

    def ag_pass(p, up):
        k, lo, hi = PARTS[p]
        i = 0 if up else 1
        rows = g.at[k, lo:hi, y_down if up else y_up, i]
        return remote(rows, rows, af_s.at[p, i], af_r.at[p, i], at_row(y_up if up else y_down, xh))

    def ag_pass_wait(p, up):
        k, lo, hi = PARTS[p]
        i = 0 if up else 1
        rows = g.at[k, lo:hi, (y + 2) % 4, i]
        remote(rows, rows, af_s.at[p, i], af_r.at[p, i], at_row(y_up, xh)).wait_recv()

    def ag_start(p):
        for up in (True, False):
            ag_own(p, up).start()

    def ag_middle(p):
        for up in (True, False):
            ag_own_wait(p, up)
            ag_pass(p, up).start()

    def ag_end(p):
        for up in (True, False):
            ag_pass_wait(p, up)

    src = block(0, 1 - xl, c)
    remote(src, src, x0_s, x0_r, at_depth(dep_x)).wait_recv()
    to_core(0, 1 - xl, cf_s, cf_r).start()
    arrive_pair(1, xl, *own_sems)
    stage_products(0)
    arrive_pair(1, 1 - xl, *far_sems)
    arrive_pair(2, xl, *own_sems)
    stage_products(1)
    arrive_pair(2, 1 - xl, *far_sems)
    arrive_pair(3, xl, *own_sems)
    stage_y(0)
    stage_products(2)
    arrive_pair(3, 1 - xl, *far_sems)
    arrive_last(xl, *own_sems)
    stage_x(0)
    stage_products(3)
    stage_y(1)
    arrive_last(1 - xl, *far_sems)
    stage_products(4)
    stage_x(1)
    stage_y(2)
    for k in range(GU):
        w2t[k * LANES : (k + 1) * LANES, :] = w2[:, k * LANES : (k + 1) * LANES].T
    stage_x(2)
    stage_y(3)
    for q in range(3):
        ag_x_wait(q)
    for p in range(4):
        ag_start(p)
    stage_x(3)
    stage_y(4)
    stage_x(4)
    ag_x_hidden(xh).start()
    for p in range(4):
        ag_middle(p)
    for q in (3, 4):
        ag_x_wait(q)

    def piece(k, j):
        d = (dep + j) % DEEP
        return remote(piece_send.at[k, d], piece_recv.at[k, dep], p_s.at[k, j], p_r.at[k, j], at_depth(d))

    def piece_wait(k, j):
        dst = piece_recv.at[k, (dep + DEEP - j) % DEEP]
        remote(dst, dst, p_s.at[k, j], p_r.at[k, j], at_depth(dep_x)).wait_recv()

    def pieces(k):
        gk = g[k].reshape(1024, LANES)
        piece_send[k] = mm(xt[...].reshape(WIDE, 1024), gk).astype(BF16).reshape(DEEP, PIECE, LANES)

    def pieces_start(k):
        for j in (2, 1, 3):
            piece(k, j).start()
        piece_recv[k, dep] = piece_send[k, dep]

    def ig_group(q):
        lo, hi = GROUPS[q]
        r = 0.0
        for k in range(GU):
            r = r + mm(g[k, lo:hi].reshape((hi - lo) * 128, LANES), w2t[k * LANES : (k + 1) * LANES, :])
        r = r.reshape(hi - lo, 2, 2, ROWS, WIDE)
        for s in range(lo, hi):
            for a in range(2):
                for b in range(2):
                    ig[b, a, s] = r[s - lo, a, b]
        ig_c(q).start()

    def ig_c(q):
        lo, hi = GROUPS[q]
        return remote(ig.at[1 - c, :, lo:hi], ig_core.at[:, lo:hi], ic_s.at[q], ic_r.at[q], at_depth(dep_c))

    def ig_z(s):
        return remote(ig_zs.at[s], ig_zr.at[s], iz_s.at[s], iz_r.at[s], at_col((z + DELTA[s] + STEPS) % STEPS))

    def ig_chip(q):
        lo, hi = GROUPS[q]
        ig_c(q).wait_recv()
        for s in range(lo, hi):
            total = ig[c, :, s] + ig_core[:, s]
            if s:
                ig_zs[s] = total.astype(BF16)
                ig_z(s).start()
            else:
                ig_fin[...] = total

    for p in range(4, 8):
        ag_start(p)
    for p in range(4):
        ag_end(p)
    ig_group(2)
    ag_middle(4)
    ag_middle(5)
    ig_group(1)
    ag_middle(6)
    ag_middle(7)
    ag_x_hidden(1 - xh).wait_recv()
    ag_start(8)
    ag_start(9)
    ag_end(4)
    pieces(0)
    pieces_start(0)
    ig_chip(2)
    ig_group(0)
    ag_end(5)
    pieces(1)
    pieces_start(1)
    ig_chip(1)
    ig_chip(0)
    ag_end(6)
    ag_end(7)
    ig_group(4)
    ig_group(3)
    pieces(2)
    pieces_start(2)
    ig_chip(4)
    ig_chip(3)
    pieces(3)
    pieces_start(3)
    ag_middle(8)
    ag_middle(9)

    ag_end(8)
    ag_end(9)

    def down_step(t, carry):
        h = g[GU + t].reshape(1024, LANES)
        r = lax.dot_general(h, xd[1].reshape(1024, WIDE), (((0,), (0,)), ((), ())), preferred_element_type=F32)
        down[pl.ds(pl.multiple_of(t * LANES, LANES), LANES), :] = r.astype(BF16)
        return carry

    lax.fori_loop(0, 2, down_step, 0)
    outs = [pltpu.make_async_copy(down.at[pl.ds(0, OWN)], down_out, out_sem.at[0])]
    outs[0].start()

    def assemble(k):
        for j in (1, 2, 3):
            piece_wait(k, j)
        wide = min(CUT, OWN - k * CUT)
        for src in range(DEEP):
            lanes = slice(src * OWN + k * CUT, src * OWN + k * CUT + wide)
            gate_fin[:, lanes] = piece_recv[k, src, :, 0:wide]
            up_fin[:, lanes] = piece_recv[k, src, :, CUT : CUT + wide]

    to_x().wait_send()
    diagonal(1).wait_send()
    diagonal(2).wait_send()
    for a, zs, zr, cs, cr in ((xl, *own_sems), (1 - xl, *far_sems)):
        ring_last(a, zs, zr, 0).wait_send()
        ring_last(a, zs, zr, 1).wait_send()

        for s in range(1 if zs is zo_s else 3, 7):
            ring(s, a, zs, zr).wait_send()
        for s in range(STEPS):
            to_core(s, a, cs, cr).wait_send()

    ag_x_hidden(xh).wait_send()
    for q in range(len(GROUPS)):
        for j in (1, 2, 3):
            y_send(q, j).wait_send()
        x_send(q).wait_send()
        ag_x(q).wait_send()
    assemble(0)
    for p in range(len(PARTS)):
        for up in (True, False):
            ag_own(p, up).wait_send()
            ag_pass(p, up).wait_send()
    assemble(1)
    total = ig_fin[...]
    for s in range(1, STEPS):
        ig_z(s).wait_recv()
        total = total + ig_zr[s].astype(F32)
    ig_fin[...] = total

    ig_xs[...] = ig_fin[1 - xl].astype(BF16)
    ig_x = remote(ig_xs, ig_xr, ix_s, ix_r, at_depth(dep_x))
    ig_x.start()
    assemble(2)
    ig_x.wait_recv()
    ig_res[...] = (ig_fin[xl] + ig_xr[...].astype(F32)).astype(BF16)
    outs.append(pltpu.make_async_copy(ig_res, ig_out, out_sem.at[3]))
    outs[-1].start()
    assemble(3)
    for i, (src, dst) in enumerate(((gate_fin, gate_out), (up_fin, up_out))):
        outs.append(pltpu.make_async_copy(src, dst, out_sem.at[1 + i]))
        outs[-1].start()

    for k in range(GU):
        for j in (1, 2, 3):
            piece(k, j).wait_send()
    for q in range(len(GROUPS)):
        ig_c(q).wait_send()
    ig_x.wait_send()
    for s in range(1, STEPS):
        ig_z(s).wait_send()
    for cp in outs:
        cp.wait()


def hand_on(a0, a1, a2, a3, b0, b1, b2, b3, v0, v1, v2, v3, sem_in, sem_out):
    sets = ((a1, v1, b1), (a2, v2, b2), (a3, v3, b3), (a0, v0, b0))
    loads = [pltpu.make_async_copy(a, v, sem_in.at[i]) for i, (a, v, b) in enumerate(sets)]
    stores = [pltpu.make_async_copy(v, b, sem_out.at[i]) for i, (a, v, b) in enumerate(sets)]
    for cp in loads:
        cp.start()
    for load, store in zip(loads, stores):
        load.wait()
        store.start()
    for cp in stores:
        cp.wait()


def on_device(inputs, out_grad, w_gate, w_up, w_down):
    vm = pltpu.VMEM
    dma = pltpu.SemaphoreType.DMA
    anyspace = pl.BlockSpec(memory_space=pl.ANY)
    shapes = (
        jax.ShapeDtypeStruct((ROWS, WIDE), BF16),
        jax.ShapeDtypeStruct((PIECE, FULL), BF16),
        jax.ShapeDtypeStruct((PIECE, FULL), BF16),
        jax.ShapeDtypeStruct((OWN, WIDE), BF16),
    )
    results = pl.pallas_call(
        kernel,
        out_shape=shapes,
        in_specs=[anyspace] * 5,
        out_specs=(anyspace,) * 4,
        scratch_shapes=[
            vm((2, STEPS, 2, 2, ROWS, WIDE), BF16),
            vm((DEEP, PIECE, 1024), BF16),
            vm((2, WIDE, WIN), BF16),
            vm((WIDE, 2 * PAD), BF16),
            vm((2 * PAD, WIDE), BF16),
            vm((PAD, WIDE), BF16),
            vm((DEEP, 2, ROWS, SUMS), F32),
            vm((STEPS, ROWS, SUMS), F32),
            vm((DEEP, STEPS, ROWS, SUMS), BF16),
            vm((3, STEPS, ROWS, SUMS), BF16),
            vm((2, STEPS, HALF, SUMS), F32),
            vm((STEPS, HALF, SUMS), F32),
            vm((CHUNKS, STEPS, 4, 2, HALF, LANES), BF16),
            vm((GU, DEEP, PIECE, LANES), BF16),
            vm((GU, DEEP, PIECE, LANES), BF16),
            vm((PIECE, FULL), BF16),
            vm((PIECE, FULL), BF16),
            vm((PAD, WIDE), BF16),
            vm((2, 2, STEPS, ROWS, WIDE), F32),
            vm((2, STEPS, ROWS, WIDE), F32),
            vm((ROWS, WIDE), BF16),
            vm((ROWS, WIDE), BF16),
            vm((STEPS, 2, ROWS, WIDE), BF16),
            vm((STEPS, 2, ROWS, WIDE), BF16),
            vm((2, ROWS, WIDE), F32),
            vm((ROWS, WIDE), BF16),
            dma((5,)),
            dma((9,)), dma((9,)),
            dma((9,)), dma((9,)),
            dma((8,)), dma((8,)),
            dma((8,)), dma((8,)),
            dma, dma,
            dma((5, 3)), dma((5, 3)),
            dma((5,)), dma((5,)),
            dma((6,)), dma((6,)),
            dma((10, 2)), dma((10, 2)),
            dma((10, 2)), dma((10, 2)),
            dma((GU, 4)), dma((GU, 4)),
            dma((5,)), dma((5,)),
            dma, dma,
            dma((8,)), dma((8,)),
            dma((4,)),
        ],
        compiler_params=pltpu.CompilerParams(
            collective_id=0, has_side_effects=True, vmem_limit_bytes=60 * 1024 * 1024
        ),
        cost_estimate=pl.CostEstimate(flops=8 * 10**9, bytes_accessed=12 * 10**6, transcendentals=10**6),
        name="ffn_backward",
    )(inputs, out_grad, w_gate, w_up, w_down)
    return pl.pallas_call(
        hand_on,
        out_shape=shapes,
        in_specs=[anyspace] * 4,
        out_specs=(anyspace,) * 4,
        scratch_shapes=[vm(a.shape, BF16) for a in shapes] + [dma((4,)), dma((4,))],
        name="hand_on",
    )(*results)


def solution(mesh):
    placed = (
        P(("depth", "col"), "row"),
        P(("depth", "col"), "row"),
        P("row", "col"),
        P("row", "col"),
        P("col", "row"),
    )
    return jax.shard_map(
        on_device,
        mesh=mesh,
        in_specs=placed,
        out_specs=(
            P(("depth", "col"), "row"),
            P(("row", "depth"), "col"),
            P(("row", "depth"), "col"),
            P(("col", "depth"), "row"),
        ),
        check_vma=False,
    )
```

```python
import jax
import jax.numpy as jnp
from jax import lax
from jax.experimental import pallas as pl
from jax.experimental.pallas import tpu as pltpu
from jax.sharding import PartitionSpec as P

MESH = pl.DeviceIdType.MESH
F32, BF16 = jnp.float32, jnp.bfloat16

DELTA = (0, 1, -1, 2, -2, 3, -3, 4)
DEEP = 4
STEPS = 8
ROWS = 32
WIDE = 896
FULL = 1920
OWN = 480
PAD = 512
WIN = 640
PIECE = 224
HALF = ROWS // 2
CUT = 128
GU = 4
CHUNKS = 6
LANES = 2 * CUT
SUMS = 3 * PAD
GROUPS = ((0, 1), (1, 3), (3, 5), (5, 7), (7, 8))
PARTS = tuple((k, 0, 5) for k in range(4)) + tuple((k, 5, 8) for k in range(4)) + ((4, 0, 8), (5, 0, 8))


def mm(a, b):
    return lax.dot_general(a, b, (((1,), (0,)), ((), ())), preferred_element_type=F32)


def mm_t(a, b):
    return lax.dot_general(a, b, (((1,), (1,)), ((), ())), preferred_element_type=F32)


def kernel(
    x_hbm, dy_hbm, wg_hbm, wu_hbm, wd_hbm,
    ig_out, gate_out, up_out, down_out,
    xd, xt, win, w2, w2t, wd, part, part_own, psend, precv, ysum, xrecv, g,
    piece_send, piece_recv, gate_fin, up_fin, down, ig, ig_core, ig_xs, ig_xr, ig_zs, ig_zr, ig_fin, ig_res,
    load_sem, zo_s, zo_r, zf_s, zf_r, co_s, co_r, cf_s, cf_r, x0_s, x0_r, y_s, y_r, h_s, h_r,
    ah_s, ah_r, ay_s, ay_r, af_s, af_r, p_s, p_r, ic_s, ic_r, ix_s, ix_r, iz_s, iz_r, out_sem,
):
    row, z, dep = lax.axis_index("row"), lax.axis_index("col"), lax.axis_index("depth")
    y, xh = row // 2, row % 2
    xl, c = dep // 2, dep % 2
    dep_x = (1 - xl) * 2 + c
    dep_c = xl * 2 + 1 - c
    dep_xc = (1 - xl) * 2 + 1 - c
    y_up, y_down = (y + 1) % 4, (y + 3) % 4

    def at_row(yy, hh):
        return {"row": yy * 2 + hh, "col": z, "depth": dep}

    def at_depth(d):
        return {"row": row, "col": z, "depth": d}

    def at_col(zz):
        return {"row": row, "col": zz, "depth": dep}

    x_peer = at_row(y, 1 - xh)

    def remote(src, dst, ss, rs, dev):
        return pltpu.make_async_remote_copy(
            src_ref=src, dst_ref=dst, send_sem=ss, recv_sem=rs, device_id=dev, device_id_type=MESH
        )

    start = jnp.where(dep == 3, 1280, dep * 480 - (dep * 480) % 128)
    start = pl.multiple_of(start, 128)
    shift = dep * 480 - start
    loads = [
        pltpu.make_async_copy(x_hbm, xd.at[0, 0, xl, c], load_sem.at[0]),
        pltpu.make_async_copy(dy_hbm, xd.at[1, 0, xl, c], load_sem.at[1]),
        pltpu.make_async_copy(wg_hbm.at[:, pl.ds(start, WIN)], win.at[0], load_sem.at[2]),
        pltpu.make_async_copy(wu_hbm.at[:, pl.ds(start, WIN)], win.at[1], load_sem.at[3]),
        pltpu.make_async_copy(wd_hbm.at[pl.ds(dep * OWN, OWN)], wd.at[pl.ds(0, OWN)], load_sem.at[4]),
    ]
    for cp in loads:
        cp.start()

    barrier = pltpu.get_barrier_semaphore()
    peers = [at_depth(dep_x), at_depth(dep_c), at_depth(dep_xc)]
    peers += [at_col((z + m) % STEPS) for m in range(1, STEPS)]
    peers += [at_row((y + m) % 4, xh) for m in (1, 2, 3)] + [x_peer]
    peers += [{"row": row, "col": (z + m) % STEPS, "depth": dep_x} for m in (1, STEPS - 1)]
    for dev in peers:
        pl.semaphore_signal(barrier, inc=1, device_id=dev, device_id_type=MESH)

    pick = (
        lax.broadcasted_iota(jnp.int32, (WIN, PAD), 0) - lax.broadcasted_iota(jnp.int32, (WIN, PAD), 1) == shift
    ) & (lax.broadcasted_iota(jnp.int32, (WIN, PAD), 1) < OWN)
    pick = jnp.where(pick, 1.0, 0.0).astype(BF16)

    def select(i):
        loads[2 + i].wait()

        def one(t, carry):
            r = pl.ds(pl.multiple_of(t * 224, 32), 224)
            cut = mm(win[i, r], pick).astype(BF16)
            for k in range(GU):
                w2[r, k * LANES + i * CUT : k * LANES + (i + 1) * CUT] = cut[:, k * CUT : (k + 1) * CUT]
            return carry

        lax.fori_loop(0, 4, one, 0)

    loads[0].wait()
    loads[1].wait()
    pl.semaphore_wait(barrier, len(peers))

    def block(s, a, b):
        return xd.at[:, s, a, b]

    def ring(s, a, ss, rs):
        to = (z + STEPS - 1) % STEPS if s % 2 else (z + 1) % STEPS
        return remote(block(max(s - 2, 0), a, c), block(s, a, c), ss.at[s], rs.at[s], at_col(to))

    def ring_last(a, ss, rs, i):
        to = (z + 1) % STEPS if i == 0 else (z + STEPS - 1) % STEPS
        src = 6 if i == 0 else 5
        return remote(xd.at[i, src, a, c], xd.at[i, 7, a, c], ss.at[7 + i], rs.at[7 + i], at_col(to))

    def to_core(s, a, ss, rs):
        return remote(block(s, a, c), block(s, a, c), ss.at[s], rs.at[s], at_depth(dep_c))

    def to_x():
        return remote(block(0, xl, c), block(0, xl, c), x0_s, x0_r, at_depth(dep_x))

    def diagonal(s):
        to = (z + STEPS - 1) % STEPS if s == 1 else (z + 1) % STEPS
        dev = {"row": row, "col": to, "depth": dep_x}
        return remote(block(0, xl, c), block(s, xl, c), zf_s.at[s], zf_r.at[s], dev)

    to_x().start()
    to_core(0, xl, co_s, co_r).start()
    ring(1, xl, zo_s, zo_r).start()
    ring(2, xl, zo_s, zo_r).start()
    diagonal(1).start()
    diagonal(2).start()

    select(0)
    select(1)
    loads[4].wait()
    wd[OWN:PAD, :] = jnp.zeros((PAD - OWN, WIDE), BF16)

    def arrive_pair(m, a, zs, zr, cs, cr):
        for s in (2 * m - 1, 2 * m):
            ring(s, a, zs, zr).wait_recv()
            if m < 3:
                ring(s + 2, a, zs, zr).start()
            else:
                ring_last(a, zs, zr, s % 2).start()
        for s in (2 * m - 1, 2 * m):
            to_core(s, a, cs, cr).start()

    def arrive_last(a, zs, zr, cs, cr):
        ring_last(a, zs, zr, 0).wait_recv()
        ring_last(a, zs, zr, 1).wait_recv()
        to_core(7, a, cs, cr).start()

    own_sems = (zo_s, zo_r, co_s, co_r)
    far_sems = (zf_s, zf_r, cf_s, cf_r)

    def y_send(q, j):
        d = (y + 4 - j) % 4
        rows = pl.ds(GROUPS[q][0], GROUPS[q][1] - GROUPS[q][0])
        return remote(psend.at[d, rows], precv.at[j - 1, rows], y_s.at[q, j - 1], y_r.at[q, j - 1], at_row(d, xh))

    def x_send(q):
        rows = pl.ds(GROUPS[q][0], GROUPS[q][1] - GROUPS[q][0])
        return remote(ysum.at[1 - xh, rows], xrecv.at[rows], h_s.at[q], h_r.at[q], x_peer)

    def ag_x(q):
        lo, hi = GROUPS[q]
        rows = g.at[0:GU, lo:hi, y, xh]
        return remote(rows, rows, ah_s.at[q], ah_r.at[q], x_peer)

    def ag_x_wait(q):
        lo, hi = GROUPS[q]
        rows = g.at[0:GU, lo:hi, y, 1 - xh]
        remote(rows, rows, ah_s.at[q], ah_r.at[q], x_peer).wait_recv()

    def ag_x_hidden(half):
        rows = g.at[GU:CHUNKS, :, y, half]
        return remote(rows, rows, ah_s.at[5], ah_r.at[5], x_peer)

    def stage_products(q):
        lo, hi = GROUPS[q]
        n = hi - lo
        for s in range(lo, hi):
            to_core(s, xl, co_s, co_r).wait_recv()
            to_core(s, 1 - xl, cf_s, cf_r).wait_recv()
        xs = xd[0, lo:hi].reshape(n * 128, WIDE)
        ds = xd[1, lo:hi].reshape(n * 128, WIDE)
        for a, b, p in ((0, 2 * PAD, mm(xs, w2[...])), (2 * PAD, SUMS, mm_t(ds, wd[...]))):
            p = p.reshape(n, DEEP, ROWS, b - a)
            for s in range(n):
                part[:, s, :, a:b] = p[s]
                psend[:, lo + s, :, a:b] = p[s].astype(BF16)
        for j in (2, 1, 3):
            y_send(q, j).start()
        part_own[lo:hi] = part[y, 0:n]
        for s in range(lo, hi):
            xt[:, :, s * 128 : (s + 1) * 128] = xd[0, s].reshape(128, WIDE).T.reshape(DEEP, PIECE, 128)

    def stage_y(q):
        lo, hi = GROUPS[q]
        for j in (1, 3, 2):
            y_send(q, j).wait_recv()
        for s in range(lo, hi):
            total = part_own[s]
            for j in (1, 3, 2):
                total = total + precv[j - 1, s].astype(F32)
            total = total.reshape(2, HALF, SUMS)
            ysum[0, s] = total[0]
            ysum[1, s] = total[1]
        x_send(q).start()

    def stage_x(q):
        lo, hi = GROUPS[q]
        x_send(q).wait_recv()
        for s in range(lo, hi):
            total = ysum[xh, s] + xrecv[s]
            for k in range(GU):
                gate = total[:, k * LANES : k * LANES + CUT]
                up = total[:, k * LANES + CUT : (k + 1) * LANES]
                back = total[:, 2 * PAD + k * CUT : 2 * PAD + (k + 1) * CUT]
                sigma = jax.nn.sigmoid(gate)
                lanes = slice((k % 2) * CUT, (k % 2 + 1) * CUT)
                g[GU + k // 2, s, y, xh, :, lanes] = (gate * sigma * up).astype(BF16)
                g[k, s, y, xh, :, 0:CUT] = (back * up * sigma * (1.0 + gate * (1.0 - sigma))).astype(BF16)
                g[k, s, y, xh, :, CUT:LANES] = (back * gate * sigma).astype(BF16)
        ag_x(q).start()

    def ag_own(p, up):
        k, lo, hi = PARTS[p]
        rows = g.at[k, lo:hi, y]
        i = 0 if up else 1
        return remote(rows, rows, ay_s.at[p, i], ay_r.at[p, i], at_row(y_up if up else y_down, xh))

    def ag_own_wait(p, up):
        k, lo, hi = PARTS[p]
        rows = g.at[k, lo:hi, y_down if up else y_up]
        i = 0 if up else 1
        remote(rows, rows, ay_s.at[p, i], ay_r.at[p, i], at_row(y_up, xh)).wait_recv()

    def ag_pass(p, up):
        k, lo, hi = PARTS[p]
        i = 0 if up else 1
        rows = g.at[k, lo:hi, y_down if up else y_up, i]
        return remote(rows, rows, af_s.at[p, i], af_r.at[p, i], at_row(y_up if up else y_down, xh))

    def ag_pass_wait(p, up):
        k, lo, hi = PARTS[p]
        i = 0 if up else 1
        rows = g.at[k, lo:hi, (y + 2) % 4, i]
        remote(rows, rows, af_s.at[p, i], af_r.at[p, i], at_row(y_up, xh)).wait_recv()

    def ag_start(p):
        for up in (True, False):
            ag_own(p, up).start()

    def ag_middle(p):
        for up in (True, False):
            ag_own_wait(p, up)
            ag_pass(p, up).start()

    def ag_end(p):
        for up in (True, False):
            ag_pass_wait(p, up)

    src = block(0, 1 - xl, c)
    remote(src, src, x0_s, x0_r, at_depth(dep_x)).wait_recv()
    to_core(0, 1 - xl, cf_s, cf_r).start()
    arrive_pair(1, xl, *own_sems)
    stage_products(0)
    arrive_pair(1, 1 - xl, *far_sems)
    arrive_pair(2, xl, *own_sems)
    stage_products(1)
    arrive_pair(2, 1 - xl, *far_sems)
    arrive_pair(3, xl, *own_sems)
    stage_y(0)
    stage_products(2)
    arrive_pair(3, 1 - xl, *far_sems)
    arrive_last(xl, *own_sems)
    stage_x(0)
    stage_products(3)
    stage_y(1)
    arrive_last(1 - xl, *far_sems)
    stage_products(4)
    stage_x(1)
    stage_y(2)
    for k in range(GU):
        w2t[k * LANES : (k + 1) * LANES, :] = w2[:, k * LANES : (k + 1) * LANES].T
    stage_x(2)
    stage_y(3)
    for q in range(3):
        ag_x_wait(q)
    for p in range(4):
        ag_start(p)
    stage_x(3)
    stage_y(4)
    stage_x(4)
    ag_x_hidden(xh).start()
    for p in range(4):
        ag_middle(p)
    for q in (3, 4):
        ag_x_wait(q)

    def piece(k, j):
        d = (dep + j) % DEEP
        return remote(piece_send.at[k, d], piece_recv.at[k, dep], p_s.at[k, j], p_r.at[k, j], at_depth(d))

    def piece_wait(k, j):
        dst = piece_recv.at[k, (dep + DEEP - j) % DEEP]
        remote(dst, dst, p_s.at[k, j], p_r.at[k, j], at_depth(dep_x)).wait_recv()

    def pieces(k):
        gk = g[k].reshape(1024, LANES)
        piece_send[k] = mm(xt[...].reshape(WIDE, 1024), gk).astype(BF16).reshape(DEEP, PIECE, LANES)

    def pieces_start(k):
        for j in (2, 1, 3):
            piece(k, j).start()
        piece_recv[k, dep] = piece_send[k, dep]

    def ig_group(q):
        lo, hi = GROUPS[q]
        r = 0.0
        for k in range(GU):
            r = r + mm(g[k, lo:hi].reshape((hi - lo) * 128, LANES), w2t[k * LANES : (k + 1) * LANES, :])
        r = r.reshape(hi - lo, 2, 2, ROWS, WIDE)
        for s in range(lo, hi):
            for a in range(2):
                for b in range(2):
                    ig[b, a, s] = r[s - lo, a, b]
        ig_c(q).start()

    def ig_c(q):
        lo, hi = GROUPS[q]
        return remote(ig.at[1 - c, :, lo:hi], ig_core.at[:, lo:hi], ic_s.at[q], ic_r.at[q], at_depth(dep_c))

    def ig_z(s):
        return remote(ig_zs.at[s], ig_zr.at[s], iz_s.at[s], iz_r.at[s], at_col((z + DELTA[s] + STEPS) % STEPS))

    def ig_chip(q):
        lo, hi = GROUPS[q]
        ig_c(q).wait_recv()
        for s in range(lo, hi):
            total = ig[c, :, s] + ig_core[:, s]
            if s:
                ig_zs[s] = total.astype(BF16)
                ig_z(s).start()
            else:
                ig_fin[...] = total

    for p in range(4, 8):
        ag_start(p)
    for p in range(4):
        ag_end(p)
    ig_group(2)
    ag_middle(4)
    ag_middle(5)
    ig_group(1)
    ag_middle(6)
    ag_middle(7)
    ag_x_hidden(1 - xh).wait_recv()
    ag_start(8)
    ag_start(9)
    ag_end(4)
    pieces(0)
    pieces_start(0)
    ig_chip(2)
    ig_group(0)
    ag_end(5)
    pieces(1)
    pieces_start(1)
    ig_chip(1)
    ig_chip(0)
    ag_end(6)
    ag_end(7)
    ig_group(4)
    ig_group(3)
    pieces(2)
    pieces_start(2)
    ig_chip(4)
    ig_chip(3)
    pieces(3)
    pieces_start(3)
    ag_middle(8)
    ag_middle(9)

    ag_end(8)
    ag_end(9)

    def down_step(t, carry):
        h = g[GU + t].reshape(1024, LANES)
        r = lax.dot_general(h, xd[1].reshape(1024, WIDE), (((0,), (0,)), ((), ())), preferred_element_type=F32)
        down[pl.ds(pl.multiple_of(t * LANES, LANES), LANES), :] = r.astype(BF16)
        return carry

    lax.fori_loop(0, 2, down_step, 0)
    outs = [pltpu.make_async_copy(down.at[pl.ds(0, OWN)], down_out, out_sem.at[0])]
    outs[0].start()

    def assemble(k):
        for j in (1, 2, 3):
            piece_wait(k, j)
        wide = min(CUT, OWN - k * CUT)
        for src in range(DEEP):
            lanes = slice(src * OWN + k * CUT, src * OWN + k * CUT + wide)
            gate_fin[:, lanes] = piece_recv[k, src, :, 0:wide]
            up_fin[:, lanes] = piece_recv[k, src, :, CUT : CUT + wide]

    to_x().wait_send()
    diagonal(1).wait_send()
    diagonal(2).wait_send()
    for a, zs, zr, cs, cr in ((xl, *own_sems), (1 - xl, *far_sems)):
        ring_last(a, zs, zr, 0).wait_send()
        ring_last(a, zs, zr, 1).wait_send()

        for s in range(1 if zs is zo_s else 3, 7):
            ring(s, a, zs, zr).wait_send()
        for s in range(STEPS):
            to_core(s, a, cs, cr).wait_send()

    ag_x_hidden(xh).wait_send()
    for q in range(len(GROUPS)):
        for j in (1, 2, 3):
            y_send(q, j).wait_send()
        x_send(q).wait_send()
        ag_x(q).wait_send()
    assemble(0)
    for p in range(len(PARTS)):
        for up in (True, False):
            ag_own(p, up).wait_send()
            ag_pass(p, up).wait_send()
    assemble(1)
    total = ig_fin[...]
    for s in range(1, STEPS):
        ig_z(s).wait_recv()
        total = total + ig_zr[s].astype(F32)
    ig_fin[...] = total

    ig_xs[...] = ig_fin[1 - xl].astype(BF16)
    ig_x = remote(ig_xs, ig_xr, ix_s, ix_r, at_depth(dep_x))
    ig_x.start()
    assemble(2)
    ig_x.wait_recv()
    ig_res[...] = (ig_fin[xl] + ig_xr[...].astype(F32)).astype(BF16)
    outs.append(pltpu.make_async_copy(ig_res, ig_out, out_sem.at[3]))
    outs[-1].start()
    assemble(3)
    for i, (src, dst) in enumerate(((gate_fin, gate_out), (up_fin, up_out))):
        outs.append(pltpu.make_async_copy(src, dst, out_sem.at[1 + i]))
        outs[-1].start()

    for k in range(GU):
        for j in (1, 2, 3):
            piece(k, j).wait_send()
    for q in range(len(GROUPS)):
        ig_c(q).wait_send()
    ig_x.wait_send()
    for s in range(1, STEPS):
        ig_z(s).wait_send()
    for cp in outs:
        cp.wait()


def hand_on(a0, a1, a2, a3, b0, b1, b2, b3, v0, v1, v2, v3, sem_in, sem_out):
    sets = ((a1, v1, b1), (a2, v2, b2), (a3, v3, b3), (a0, v0, b0))
    loads = [pltpu.make_async_copy(a, v, sem_in.at[i]) for i, (a, v, b) in enumerate(sets)]
    stores = [pltpu.make_async_copy(v, b, sem_out.at[i]) for i, (a, v, b) in enumerate(sets)]
    for cp in loads:
        cp.start()
    for load, store in zip(loads, stores):
        load.wait()
        store.start()
    for cp in stores:
        cp.wait()


def on_device(inputs, out_grad, w_gate, w_up, w_down):
    vm = pltpu.VMEM
    dma = pltpu.SemaphoreType.DMA
    anyspace = pl.BlockSpec(memory_space=pl.ANY)
    shapes = (
        jax.ShapeDtypeStruct((ROWS, WIDE), BF16),
        jax.ShapeDtypeStruct((PIECE, FULL), BF16),
        jax.ShapeDtypeStruct((PIECE, FULL), BF16),
        jax.ShapeDtypeStruct((OWN, WIDE), BF16),
    )
    results = pl.pallas_call(
        kernel,
        out_shape=shapes,
        in_specs=[anyspace] * 5,
        out_specs=(anyspace,) * 4,
        scratch_shapes=[
            vm((2, STEPS, 2, 2, ROWS, WIDE), BF16),
            vm((DEEP, PIECE, 1024), BF16),
            vm((2, WIDE, WIN), BF16),
            vm((WIDE, 2 * PAD), BF16),
            vm((2 * PAD, WIDE), BF16),
            vm((PAD, WIDE), BF16),
            vm((DEEP, 2, ROWS, SUMS), F32),
            vm((STEPS, ROWS, SUMS), F32),
            vm((DEEP, STEPS, ROWS, SUMS), BF16),
            vm((3, STEPS, ROWS, SUMS), BF16),
            vm((2, STEPS, HALF, SUMS), F32),
            vm((STEPS, HALF, SUMS), F32),
            vm((CHUNKS, STEPS, 4, 2, HALF, LANES), BF16),
            vm((GU, DEEP, PIECE, LANES), BF16),
            vm((GU, DEEP, PIECE, LANES), BF16),
            vm((PIECE, FULL), BF16),
            vm((PIECE, FULL), BF16),
            vm((PAD, WIDE), BF16),
            vm((2, 2, STEPS, ROWS, WIDE), F32),
            vm((2, STEPS, ROWS, WIDE), F32),
            vm((ROWS, WIDE), BF16),
            vm((ROWS, WIDE), BF16),
            vm((STEPS, 2, ROWS, WIDE), BF16),
            vm((STEPS, 2, ROWS, WIDE), BF16),
            vm((2, ROWS, WIDE), F32),
            vm((ROWS, WIDE), BF16),
            dma((5,)),
            dma((9,)), dma((9,)),
            dma((9,)), dma((9,)),
            dma((8,)), dma((8,)),
            dma((8,)), dma((8,)),
            dma, dma,
            dma((5, 3)), dma((5, 3)),
            dma((5,)), dma((5,)),
            dma((6,)), dma((6,)),
            dma((10, 2)), dma((10, 2)),
            dma((10, 2)), dma((10, 2)),
            dma((GU, 4)), dma((GU, 4)),
            dma((5,)), dma((5,)),
            dma, dma,
            dma((8,)), dma((8,)),
            dma((4,)),
        ],
        compiler_params=pltpu.CompilerParams(
            collective_id=0, has_side_effects=True, vmem_limit_bytes=60 * 1024 * 1024
        ),
        cost_estimate=pl.CostEstimate(flops=8 * 10**9, bytes_accessed=12 * 10**6, transcendentals=10**6),
        name="ffn_backward",
    )(inputs, out_grad, w_gate, w_up, w_down)
    return pl.pallas_call(
        hand_on,
        out_shape=shapes,
        in_specs=[anyspace] * 4,
        out_specs=(anyspace,) * 4,
        scratch_shapes=[vm(a.shape, BF16) for a in shapes] + [dma((4,)), dma((4,))],
        name="hand_on",
    )(*results)


def solution(mesh):
    placed = (
        P(("depth", "col"), "row"),
        P(("depth", "col"), "row"),
        P("row", "col"),
        P("row", "col"),
        P("col", "row"),
    )
    return jax.shard_map(
        on_device,
        mesh=mesh,
        in_specs=placed,
        out_specs=(
            P(("depth", "col"), "row"),
            P(("row", "depth"), "col"),
            P(("row", "depth"), "col"),
            P(("col", "depth"), "row"),
        ),
        check_vma=False,
    )
```
